32 devices in a mesh: space: 4 (over y, x), band: 8 (over z, core).
Axes of the slice: x: 2, y: 2, z: 4, core: 2. Of those that a mesh axis runs over, the one named last changes fastest.
Arguments:
- orbitals: float32 [768, 8, 2048], P('band', 'space'), may hold values from -6 to 6
- potential: float32 [8, 2048], P('space'), may hold values from 0 to 2
Outputs:
- filtered: float32 [768, 8, 2048], P('band', 'space')
- margin: float32 [768, 768], P('band')
The draws below stay inside these ranges and needn't reach their ends.
All inputs are finite; a program needn't handle non-finite values.
Results may differ from the reference program's by a relative error of at most 0.0002.
Values sent between devices are 32-bit elements; how exact they have to be, the bound alone decides.
No kernel may reach another device: no remote copies, remote signals or barrier semaphores. Data moves between devices by JAX's collectives and lax.ppermute only.
A program may use at most 64 MiB of HBM per device.

```python
import jax
import jax.numpy as jnp
from jax import lax

ORBS = 768
NY = 32
NZ = 64
NX = 8
N_BAND = 8


def raised(array, own_key, source, target, shards_of, factor):
    owner, partner = [(jnp.arange(array.shape[position]) // (array.shape[position] // shards_of)).reshape([-1 if axis == position else 1 for axis in range(array.ndim)]) for position in (source, target)]
    chosen = jax.random.permutation(own_key, shards_of)[partner]
    strong = (owner == chosen) | (owner == (partner + shards_of // 2) % shards_of)
    return jnp.where(strong, factor * array, array)


def block_levels(rng, extent, pieces, low, largest):
    level, own = 1.0, jax.random.fold_in(rng, 6)
    for position, parts in pieces:
        steps = jnp.exp(jax.random.uniform(jax.random.fold_in(own, position), (parts,), jnp.float32, low / len(pieces), largest / len(pieces)))
        level = level * jnp.repeat(steps, extent[position] // parts).reshape([-1 if axis == position else 1 for axis in range(len(extent))])
    return level


def bell_draw_with(rng, shape, width, bound, shards, heavy, kind=jnp.bfloat16):
    drawn = width * jax.random.normal(rng, shape, jnp.float32)
    if shards:
        drawn = drawn * block_levels(rng, shape, shards, -0.22, 0.18)
    return jnp.clip(raised(drawn, jax.random.fold_in(rng, 3), *heavy), -bound, bound).astype(kind)


def setup_inputs(seed: int = 0) -> dict:
    key_of = jax.random.split(jax.random.key(seed), 3)
    return {
        "orbitals": bell_draw_with(key_of[0], (ORBS, NX, NY * NZ), 1.0, 6.0, ((0, 8), (1, 4)), (1, 0, 8, 2.0), jnp.float32),
        "potential": jnp.clip(2.0 * jax.random.uniform(key_of[1], (NX, NY * NZ), jnp.float32) ** block_levels(key_of[1], (NX, NY * NZ), ((0, 4),), -0.2, 0.2), 0.0, 2.0),
    }


def shift_plane(flat, step, depth):
    pos = lax.broadcasted_iota(jnp.int32, (flat.shape[-1],), 0) % depth
    inside = (pos + step >= 0) & (pos + step < depth)
    direct = jnp.roll(flat, -step, axis=-1)
    if step > 0:
        wrapped = jnp.roll(flat, depth - step, axis=-1)
    else:
        wrapped = jnp.roll(flat, -step - depth, axis=-1)
    return jnp.where(inside, direct, wrapped)


def plane_terms(center, depth):
    near = jnp.roll(center, -depth, axis=-1) + jnp.roll(center, depth, axis=-1)
    far = jnp.roll(center, -2 * depth, axis=-1) + jnp.roll(center, 2 * depth, axis=-1)
    near = near + shift_plane(center, 1, depth) + shift_plane(center, -1, depth)
    far = far + shift_plane(center, 2, depth) + shift_plane(center, -2, depth)
    return (4.0 / 3.0) * near - (1.0 / 12.0) * far


def apply_hamiltonian(field, potential):
    near = jnp.roll(field, 1, axis=1) + jnp.roll(field, -1, axis=1)
    far = jnp.roll(field, 2, axis=1) + jnp.roll(field, -2, axis=1)
    laplace = (4.0 / 3.0) * near - (1.0 / 12.0) * far + plane_terms(field, NZ) - 7.5 * field
    return -0.5 * laplace + potential[None] * field


def filter_block(block, potential):
    first = (apply_hamiltonian(block, potential) - 6.0 * block) / 4.0
    second = 2.0 * (apply_hamiltonian(first, potential) - 6.0 * first) / 4.0 - block
    return 2.0 * (apply_hamiltonian(second, potential) - 6.0 * second) / 4.0 - first


def reference(orbitals, potential):
    blocks = orbitals.reshape(N_BAND, ORBS // N_BAND, NX, NY * NZ)
    filtered = lax.map(lambda block: filter_block(block, potential), blocks).reshape(orbitals.shape)
    flat = filtered.reshape(ORBS, NX * NY * NZ)
    margin = jnp.dot(flat, flat.T, precision=lax.Precision.HIGHEST, preferred_element_type=jnp.float32)
    return filtered, margin * (1.0 / (NX * NY * NZ))
```

```python
import functools

import jax
import jax.numpy as jnp
from jax import lax
from jax.experimental import pallas as pl
from jax.experimental.pallas import tpu as pltpu
from jax.sharding import PartitionSpec as P

NZ = 64
LANES = 128
SUBLANES = 8


def filter_kernel(space, layers, tiles, chunk, x_pitch, v_pitch, x_ref, v_ref, out_ref, f0, r0, f1, r1, f2, r2, coef):
    planes = space * layers
    rows = tiles * layers
    lane = lax.broadcasted_iota(jnp.int32, (chunk, LANES), 1)
    depth = lane % NZ
    first_half = lane < NZ
    starts = [depth < 1, depth < 2]
    ends = [depth >= NZ - 1, depth >= NZ - 2]

    def load(tile, carry):
        for p in range(planes):
            s, l = divmod(p, layers)
            row = tile * layers + l
            v = x_ref[pl.ds(s * x_pitch * rows + row, chunk, stride=rows), :]
            f0[tile, p] = v
            r0[tile, p] = pltpu.roll(v, NZ, 1)
            w = v_ref[pl.ds((s * v_pitch + v_pitch - 1) * rows + row, 1), :]
            coef[tile, p] = jnp.broadcast_to(0.25 * w - 0.5625, (chunk, LANES))
        return carry

    def stencil(f, r, tile):
        up = jnp.where(tile == tiles - 1, 0, tile + 1)
        down = jnp.where(tile == 0, tiles - 1, tile - 1)
        v = [f[tile, p] for p in range(planes)]
        pairs = {}

        def pair(a, b):
            key = (min(a, b), max(a, b))
            if key not in pairs:
                pairs[key] = v[a] + v[b]
            return pairs[key]

        out = []
        for p in range(planes):
            rolled = r[tile, p]
            near = pair((p - 1) % planes, (p + 1) % planes)
            far = pair((p - 2) % planes, (p + 2) % planes)
            far = far + (f[up, p] + f[down, p])
            near = near + (rolled + jnp.where(first_half, r[down, p], r[up, p]))
            near = near + pltpu.roll(jnp.where(starts[0], rolled, v[p]), LANES - 1, 1)
            near = near + pltpu.roll(jnp.where(ends[0], rolled, v[p]), 1, 1)
            far = far + pltpu.roll(jnp.where(starts[1], rolled, v[p]), LANES - 2, 1)
            far = far + pltpu.roll(jnp.where(ends[1], rolled, v[p]), 2, 1)
            out.append((v[p], far - 16.0 * near))
        return out

    def first(tile, carry):
        for p, (v, s) in enumerate(stencil(f0, r0, tile)):
            y = (1.0 / 96.0) * s + coef[tile, p] * v
            f1[tile, p] = y
            r1[tile, p] = pltpu.roll(y, NZ, 1)
        return carry

    def second(tile, carry):
        for p, (v, s) in enumerate(stencil(f1, r1, tile)):
            y = 2.0 * ((1.0 / 96.0) * s + coef[tile, p] * v) - f0[tile, p]
            f2[tile, p] = y
            r2[tile, p] = pltpu.roll(y, NZ, 1)
        return carry

    def third(tile, carry):
        for p, (v, s) in enumerate(stencil(f2, r2, tile)):
            y = 2.0 * ((1.0 / 96.0) * s + coef[tile, p] * v) - f1[tile, p]
            out_ref[p // layers, tile * layers + p % layers] = y
        return carry

    for step in (load, first, second, third):
        lax.fori_loop(0, tiles, step, 0)


def run_filter(x, v, space, layers, tiles, chunk):
    rows = tiles * layers
    planes = space * layers
    x_pitch = x.shape[0] // (space * rows)
    v_pitch = v.shape[0] // (space * rows)
    field = pltpu.VMEM((tiles, planes, chunk, LANES), jnp.float32)
    return pl.pallas_call(
        functools.partial(filter_kernel, space, layers, tiles, chunk, x_pitch, v_pitch),
        out_shape=jax.ShapeDtypeStruct((space, rows, chunk, LANES), jnp.float32),
        in_specs=[pl.BlockSpec(memory_space=pltpu.VMEM)] * 2,
        out_specs=pl.BlockSpec(memory_space=pltpu.VMEM),
        scratch_shapes=[field] * 7,
        compiler_params=pltpu.CompilerParams(vmem_limit_bytes=40 * 1024 * 1024),
        cost_estimate=pl.CostEstimate(
            flops=75 * planes * rows * max(chunk, SUBLANES) * LANES // layers,
            bytes_accessed=2 * planes * tiles * chunk * LANES * 4,
            transcendentals=0,
        ),
    )(x, v)


def rotate(x, axis, step):
    size = lax.axis_size(axis)
    return lax.ppermute(x, axis, [(i, (i + step) % size) for i in range(size)])


def shards(orbitals, potential):
    space = lax.axis_size("space")
    band = lax.axis_size("band")
    count, layers, plane = orbitals.shape
    tiles = plane // LANES
    rows = tiles * layers
    share = rows // band
    own = count // space
    chunk = max(c for c in range(1, SUBLANES + 1) if own % c == 0)
    chunks = own // chunk

    spread = orbitals.reshape(count, layers, tiles, LANES).transpose(0, 2, 1, 3).reshape(count, rows, LANES)
    local_v = potential.reshape(layers, tiles, LANES).transpose(1, 0, 2).reshape(1, 1, rows, LANES)
    local_v = jnp.broadcast_to(local_v, (space, 1, rows, LANES))

    whole_v = None
    outs = []
    grams = []
    for c in range(chunks):
        part = spread[c * space * chunk : (c + 1) * space * chunk]
        if c == 0:
            part = jnp.concatenate([part.reshape(space, chunk, rows, LANES), local_v], axis=1)
            part = part.reshape(space * (chunk + 1), rows, LANES)
        got = lax.all_to_all(part, "space", split_axis=0, concat_axis=0, tiled=True)
        got = got.reshape(-1, LANES)
        if c == 0:
            whole_v = got
        filtered = run_filter(got, whole_v, space, layers, tiles, chunk)
        back = lax.all_to_all(filtered, "space", split_axis=0, concat_axis=0, tiled=True)
        outs.append(
            back.reshape(space, tiles, layers, chunk, LANES)
            .transpose(0, 3, 2, 1, 4)
            .reshape(space * chunk, layers, plane)
        )
        packed = back.reshape(space, band, share, chunk, LANES).transpose(1, 0, 2, 3, 4)
        regrouped = lax.all_to_all(packed, "band", split_axis=0, concat_axis=0, tiled=True)
        grams.append(regrouped.transpose(0, 1, 3, 2, 4).reshape(band, space * chunk, share * LANES))

    result = jnp.concatenate(outs, axis=0)
    all_orbs = jnp.concatenate(grams, axis=1)

    pairs = band // 2
    core = lax.axis_index("band") % 2
    pair = lax.axis_index("band") // 2
    mine_s = lax.axis_index("space")
    wide = all_orbs.reshape(band * count, share * LANES)
    by_core = all_orbs.reshape(pairs, 2, count, share * LANES)

    def rows_of(which):
        left = lax.dynamic_index_in_dim(by_core, which, 1, keepdims=False).reshape(pairs * count, share * LANES)
        return lax.dot_general(
            left, wide, (((1,), (1,)), ((), ())), precision=lax.Precision.HIGH, preferred_element_type=jnp.float32
        )

    other = lax.ppermute(rows_of(1 - core), "band", [(i, i ^ 1) for i in range(band)])
    total = (rows_of(core) + other).reshape(pairs, space, own, band * count)

    mine = lax.dynamic_index_in_dim(total, mine_s, 1, keepdims=False)
    for k in range(1, space):
        sent = lax.dynamic_index_in_dim(total, (mine_s + k) % space, 1, keepdims=False)
        mine = mine + rotate(sent, "space", k)

    final = lax.dynamic_index_in_dim(mine, pair, 0, keepdims=False)
    for k in range(1, pairs):
        sent = lax.dynamic_index_in_dim(mine, (pair + k) % pairs, 0, keepdims=False)
        final = final + rotate(sent, "band", 2 * k)
    final = final * (1.0 / (layers * space * plane))

    margin = jnp.zeros((space, own, band * count), jnp.float32)
    margin = lax.dynamic_update_index_in_dim(margin, final, mine_s, 0)
    for k in range(1, space):
        margin = lax.dynamic_update_index_in_dim(margin, rotate(final, "space", k), (mine_s - k) % space, 0)
    return result, margin.reshape(count, band * count)


def solution(mesh):
    return jax.shard_map(
        shards,
        mesh=mesh,
        in_specs=(P("band", "space", None), P("space", None)),
        out_specs=(P("band", "space", None), P("band", None)),
        check_vma=False,
    )
```

```python
import functools

import jax
import jax.numpy as jnp
from jax import lax
from jax.experimental import pallas as pl
from jax.experimental.pallas import tpu as pltpu
from jax.sharding import PartitionSpec as P

NZ = 64
LANES = 128
SUBLANES = 8
VMEM_LIMIT = 40 * 1024 * 1024


def unroll_of(tiles):
    return 8 if tiles % 8 == 0 else 1


def filter_kernel(space, layers, tiles, chunk, pitch, offset, planes_unroll, here_ref, x_ref, *refs):
    v_refs, out_refs = refs[:space], refs[space : 2 * space]
    f0, r0, f1, r1, f2, r2, coef = refs[2 * space :]
    planes = space * layers
    rows = tiles * layers
    lane = lax.broadcasted_iota(jnp.int32, (chunk, LANES), 1)
    depth = lane % NZ
    first_half = lane < NZ
    starts = [depth < 1, depth < 2]
    ends = [depth >= NZ - 1, depth >= NZ - 2]
    here = here_ref[0]

    def load(tile, carry):
        for p in range(planes):
            s, l = divmod(p, layers)
            row = tile * layers + l
            slab = here + s
            slab = jnp.where(slab >= space, slab - space, slab)
            v = x_ref[pl.ds((slab * pitch + offset) * rows + row, chunk, stride=rows), :]
            f0[tile, p] = v
            r0[tile, p] = pltpu.roll(v, NZ, 1)
            w = v_refs[s][pl.ds(row, 1), :]
            coef[tile, p] = jnp.broadcast_to(0.25 * w - 0.5625, (chunk, LANES))
        return carry

    def stencil(f, r, tile):
        up = jnp.where(tile == tiles - 1, 0, tile + 1)
        down = jnp.where(tile == 0, tiles - 1, tile - 1)
        v = [f[tile, p] for p in range(planes)]
        pairs = {}

        def pair(a, b):
            key = (min(a, b), max(a, b))
            if key not in pairs:
                pairs[key] = v[a] + v[b]
            return pairs[key]

        out = []
        for p in range(planes):
            rolled = r[tile, p]
            near = pair((p - 1) % planes, (p + 1) % planes)
            far = pair((p - 2) % planes, (p + 2) % planes)
            far = far + (f[up, p] + f[down, p])
            near = near + (rolled + jnp.where(first_half, r[down, p], r[up, p]))
            near = near + pltpu.roll(jnp.where(starts[0], rolled, v[p]), LANES - 1, 1)
            near = near + pltpu.roll(jnp.where(ends[0], rolled, v[p]), 1, 1)
            far = far + pltpu.roll(jnp.where(starts[1], rolled, v[p]), LANES - 2, 1)
            far = far + pltpu.roll(jnp.where(ends[1], rolled, v[p]), 2, 1)
            out.append((v[p], far - 16.0 * near))
        return out

    def first(tile, carry):
        for p, (v, s) in enumerate(stencil(f0, r0, tile)):
            y = (1.0 / 96.0) * s + coef[tile, p] * v
            f1[tile, p] = y
            r1[tile, p] = pltpu.roll(y, NZ, 1)
        return carry

    def second(tile, carry):
        for p, (v, s) in enumerate(stencil(f1, r1, tile)):
            y = 2.0 * ((1.0 / 96.0) * s + coef[tile, p] * v) - f0[tile, p]
            f2[tile, p] = y
            r2[tile, p] = pltpu.roll(y, NZ, 1)
        return carry

    def third(tile, carry):
        for p, (v, s) in enumerate(stencil(f2, r2, tile)):
            y = 2.0 * ((1.0 / 96.0) * s + coef[tile, p] * v) - f1[tile, p]
            out_refs[p // layers][tile * layers + p % layers] = y
        return carry

    for step in (load, first, second, third):
        lax.fori_loop(0, tiles, step, 0, unroll=planes_unroll)


VMEM_SPEC = pl.BlockSpec(memory_space=pltpu.VMEM)
SMEM_SPEC = pl.BlockSpec(memory_space=pltpu.SMEM)


def run_filter(here, x, vs, offset, space, layers, tiles, chunk):
    rows = tiles * layers
    planes = space * layers
    pitch = x.shape[0] // (space * rows)
    field = pltpu.VMEM((tiles, planes, chunk, LANES), jnp.float32)
    unroll = 8 if tiles % 8 == 0 and planes <= 8 else 1
    return pl.pallas_call(
        functools.partial(filter_kernel, space, layers, tiles, chunk, pitch, offset, unroll),
        out_shape=[jax.ShapeDtypeStruct((rows, chunk, LANES), jnp.float32)] * space,
        in_specs=[SMEM_SPEC] + [VMEM_SPEC] * (1 + space),
        out_specs=[VMEM_SPEC] * space,
        scratch_shapes=[field] * 7,
        compiler_params=pltpu.CompilerParams(vmem_limit_bytes=VMEM_LIMIT),
        cost_estimate=pl.CostEstimate(
            flops=75 * planes * tiles * SUBLANES * LANES,
            bytes_accessed=2 * planes * tiles * chunk * LANES * 4,
            transcendentals=0,
        ),
        name="filter",
    )(here, x, *vs)


def pack_kernel(space, band, share, chunk, subs, here_ref, *refs):
    blocks, out = refs[:-1], refs[-1]
    here = here_ref[0]
    for k in range(space):
        group = here - k
        group = jnp.where(group < 0, group + space, group)
        for sub in range(subs):
            first = pl.multiple_of((group * subs + sub) * chunk, chunk)
            block = blocks[k * subs + sub]
            for b in range(band):
                for q in range(share):
                    out[b, pl.ds(first, chunk), q * LANES : (q + 1) * LANES] = block[b * share + q]


def pack(here, blocks, space, band, share, chunk, subs):
    return pl.pallas_call(
        functools.partial(pack_kernel, space, band, share, chunk, subs),
        out_shape=jax.ShapeDtypeStruct((band, space * subs * chunk, share * LANES), jnp.float32),
        in_specs=[SMEM_SPEC] + [VMEM_SPEC] * len(blocks),
        out_specs=VMEM_SPEC,
        compiler_params=pltpu.CompilerParams(vmem_limit_bytes=VMEM_LIMIT),
        cost_estimate=pl.CostEstimate(
            flops=0, bytes_accessed=8 * band * space * subs * chunk * share * LANES, transcendentals=0
        ),
        name="pack",
    )(here, *blocks)


def unpack_kernel(space, rows, chunk, subs_of, here_ref, *refs):
    blocks, out = refs[:-1], refs[-1]
    here = here_ref[0]
    start = 0
    taken = 0
    for subs in subs_of:
        for k in range(space):
            group = here - k
            group = jnp.where(group < 0, group + space, group)
            for sub in range(subs):
                block = blocks[taken + k * subs + sub]
                first = (start + (group * subs + sub) * chunk) * rows
                for row in range(rows):
                    out[pl.ds(first + row, chunk, stride=rows), :] = block[row]
        taken += space * subs
        start += space * subs * chunk


def unpack(here, blocks, space, rows, chunk, subs_of):
    count = sum(subs_of) * space * chunk
    return pl.pallas_call(
        functools.partial(unpack_kernel, space, rows, chunk, subs_of),
        out_shape=jax.ShapeDtypeStruct((count * rows, LANES), jnp.float32),
        in_specs=[SMEM_SPEC] + [VMEM_SPEC] * len(blocks),
        out_specs=VMEM_SPEC,
        compiler_params=pltpu.CompilerParams(vmem_limit_bytes=VMEM_LIMIT),
        cost_estimate=pl.CostEstimate(flops=0, bytes_accessed=8 * count * rows * LANES, transcendentals=0),
        name="unpack",
    )(here, *blocks)


def gram_kernel(band, count, which_ref, *refs):
    parts, out, wide = refs[:-2], refs[-2], refs[-1]
    for b in range(band):
        first = b * count
        for part in parts:
            size = part.shape[1]
            wide[first : first + size, :] = part[b]
            first += size
    which = which_ref[0]
    pairs = band // 2
    picked = [wide[pl.ds(pl.multiple_of((2 * z + which) * count, SUBLANES), count), :] for z in range(pairs)]
    left = jnp.concatenate(picked, axis=0)
    left_hi = left.astype(jnp.bfloat16)
    left_lo = (left - left_hi.astype(jnp.float32)).astype(jnp.bfloat16)
    total = band * count
    step = 256 if total % 256 == 0 else total

    def dot(a, b):
        return lax.dot_general(a, b, (((1,), (1,)), ((), ())), preferred_element_type=jnp.float32)

    for c in range(0, total, step):
        right = wide[c : c + step, :]
        hi = right.astype(jnp.bfloat16)
        lo = (right - hi.astype(jnp.float32)).astype(jnp.bfloat16)
        out[:, c : c + step] = dot(left_hi, hi) + (dot(left_hi, lo) + dot(left_lo, hi))


def gram(which, parts):
    band = parts[0].shape[0]
    count = sum(p.shape[1] for p in parts)
    cells = parts[0].shape[2]
    return pl.pallas_call(
        functools.partial(gram_kernel, band, count),
        out_shape=jax.ShapeDtypeStruct((band // 2 * count, band * count), jnp.float32),
        in_specs=[SMEM_SPEC] + [VMEM_SPEC] * len(parts),
        out_specs=VMEM_SPEC,
        scratch_shapes=[pltpu.VMEM((band * count, cells), jnp.float32)],
        compiler_params=pltpu.CompilerParams(vmem_limit_bytes=VMEM_LIMIT),
        cost_estimate=pl.CostEstimate(
            flops=3 * band * band * count * count * cells,
            bytes_accessed=4 * band * count * (cells + band * count // 2),
            transcendentals=0,
        ),
        name="gram",
    )(which, *parts)


def rotate(x, axis, step):
    size = lax.axis_size(axis)
    return lax.ppermute(x, axis, [(i, (i + step) % size) for i in range(size)])


def shards(orbitals, potential):
    space = lax.axis_size("space")
    band = lax.axis_size("band")
    count, layers, plane = orbitals.shape
    tiles = plane // LANES
    rows = tiles * layers
    share = rows // band
    own = count // space
    chunk = max(c for c in range(1, SUBLANES + 1) if own % c == 0)
    chunks = own // chunk
    groups = [1] if chunks == 1 else [1, chunks - 1]

    s_index = lax.axis_index("space")
    b_index = lax.axis_index("band")
    here = s_index.reshape(1)

    def as_rows(x):
        n = x.shape[0]
        return x.reshape(n, layers, tiles, LANES).transpose(0, 2, 1, 3).reshape(n * rows, LANES)

    arrived = []
    first = 0
    for subs in groups:
        size = space * subs * chunk
        part = orbitals[first : first + size]
        first += size
        arrived.append(as_rows(lax.all_to_all(part, "space", split_axis=0, concat_axis=0, tiled=True)))

    own_v = as_rows(potential[None])
    vs = [own_v] + [rotate(own_v, "space", space - k) for k in range(1, space)]

    all_blocks = []
    parts = []
    for subs, x in zip(groups, arrived):
        made = []
        for sub in range(subs):
            outs = run_filter(here, x, vs, sub * chunk, space, layers, tiles, chunk)
            made.append([outs[0]] + [rotate(outs[k], "space", k) for k in range(1, space)])
        blocks = [made[sub][k] for k in range(space) for sub in range(subs)]
        all_blocks += blocks
        packed = pack(here, blocks, space, band, share, chunk, subs)
        parts.append(lax.all_to_all(packed, "band", split_axis=0, concat_axis=0, tiled=True))

    result = unpack(here, all_blocks, space, rows, chunk, groups)
    result = result.reshape(count, tiles, layers, LANES).transpose(0, 2, 1, 3).reshape(count, layers, plane)

    pairs = band // 2
    core = b_index % 2
    pair = b_index // 2
    other = lax.ppermute(gram((1 - core).reshape(1), parts), "band", [(i, i ^ 1) for i in range(band)])
    total = gram(core.reshape(1), parts) + other
    total = total.reshape(pairs, space, own, band * count)

    mine = lax.dynamic_index_in_dim(total, s_index, 1, keepdims=False)
    for k in range(1, space):
        sent = lax.dynamic_index_in_dim(total, (s_index + k) % space, 1, keepdims=False)
        mine = mine + rotate(sent, "space", k)

    final = lax.dynamic_index_in_dim(mine, pair, 0, keepdims=False)
    for k in range(1, pairs):
        sent = lax.dynamic_index_in_dim(mine, (pair + k) % pairs, 0, keepdims=False)
        final = final + rotate(sent, "band", 2 * k)
    final = final * (1.0 / (layers * space * plane))

    margin = jnp.zeros((space, own, band * count), jnp.float32)
    margin = lax.dynamic_update_index_in_dim(margin, final, s_index, 0)
    for k in range(1, space):
        margin = lax.dynamic_update_index_in_dim(margin, rotate(final, "space", k), (s_index - k) % space, 0)
    return result, margin.reshape(count, band * count)


def solution(mesh):
    return jax.shard_map(
        shards,
        mesh=mesh,
        in_specs=(P("band", "space", None), P("space", None)),
        out_specs=(P("band", "space", None), P("band", None)),
        check_vma=False,
    )
```

```python
import functools

import jax
import jax.numpy as jnp
from jax import lax
from jax.experimental import pallas as pl
from jax.experimental.pallas import tpu as pltpu
from jax.sharding import PartitionSpec as P

NZ = 64
LANES = 128
SUBLANES = 8
VMEM_LIMIT = 40 * 1024 * 1024


def filter_kernel(space, layers, tiles, chunk, pitch, offset, v_pitch, unroll, here_ref, x_ref, v_ref, *refs):
    out_refs = refs[:space]
    f0, r0, f1, r1, f2, r2, coef = refs[space:]
    planes = space * layers
    rows = tiles * layers
    lane = lax.broadcasted_iota(jnp.int32, (chunk, LANES), 1)
    depth = lane % NZ
    first_half = lane < NZ
    starts = [depth < 1, depth < 2]
    ends = [depth >= NZ - 1, depth >= NZ - 2]
    here = here_ref[0]

    def load(tile, carry):
        for p in range(planes):
            s, l = divmod(p, layers)
            row = tile * layers + l
            slab = here + s
            slab = jnp.where(slab >= space, slab - space, slab)
            v = x_ref[pl.ds((slab * pitch + offset) * rows + row, chunk, stride=rows), :]
            f0[tile, p] = v
            r0[tile, p] = pltpu.roll(v, NZ, 1)
            w = v_ref[pl.ds((slab * v_pitch + v_pitch - 1) * rows + row, 1), :]
            coef[tile, p] = jnp.broadcast_to(0.25 * w - 0.5625, (chunk, LANES))
        return carry

    def stencil(f, r, tile):
        up = jnp.where(tile == tiles - 1, 0, tile + 1)
        down = jnp.where(tile == 0, tiles - 1, tile - 1)
        v = [f[tile, p] for p in range(planes)]
        pairs = {}

        def pair(a, b):
            key = (min(a, b), max(a, b))
            if key not in pairs:
                pairs[key] = v[a] + v[b]
            return pairs[key]

        out = []
        for p in range(planes):
            rolled = r[tile, p]
            near = pair((p - 1) % planes, (p + 1) % planes)
            far = pair((p - 2) % planes, (p + 2) % planes)
            far = far + (f[up, p] + f[down, p])
            near = near + (rolled + jnp.where(first_half, r[down, p], r[up, p]))
            near = near + pltpu.roll(jnp.where(starts[0], rolled, v[p]), LANES - 1, 1)
            near = near + pltpu.roll(jnp.where(ends[0], rolled, v[p]), 1, 1)
            far = far + pltpu.roll(jnp.where(starts[1], rolled, v[p]), LANES - 2, 1)
            far = far + pltpu.roll(jnp.where(ends[1], rolled, v[p]), 2, 1)
            out.append((v[p], far - 16.0 * near))
        return out

    def first(tile, carry):
        for p, (v, s) in enumerate(stencil(f0, r0, tile)):
            y = (1.0 / 96.0) * s + coef[tile, p] * v
            f1[tile, p] = y
            r1[tile, p] = pltpu.roll(y, NZ, 1)
        return carry

    def second(tile, carry):
        for p, (v, s) in enumerate(stencil(f1, r1, tile)):
            y = 2.0 * ((1.0 / 96.0) * s + coef[tile, p] * v) - f0[tile, p]
            f2[tile, p] = y
            r2[tile, p] = pltpu.roll(y, NZ, 1)
        return carry

    def third(tile, carry):
        for p, (v, s) in enumerate(stencil(f2, r2, tile)):
            y = 2.0 * ((1.0 / 96.0) * s + coef[tile, p] * v) - f1[tile, p]
            out_refs[p // layers][tile * layers + p % layers] = y
        return carry

    for step in (load, first, second, third):
        lax.fori_loop(0, tiles, step, 0, unroll=unroll)


VMEM_SPEC = pl.BlockSpec(memory_space=pltpu.VMEM)
SMEM_SPEC = pl.BlockSpec(memory_space=pltpu.SMEM)


def run_filter(here, x, v, offset, space, layers, tiles, chunk):
    rows = tiles * layers
    planes = space * layers
    pitch = x.shape[0] // (space * rows)
    v_pitch = v.shape[0] // (space * rows)
    field = pltpu.VMEM((tiles, planes, chunk, LANES), jnp.float32)
    unroll = 8 if tiles % 8 == 0 and planes <= 8 else 1
    return pl.pallas_call(
        functools.partial(filter_kernel, space, layers, tiles, chunk, pitch, offset, v_pitch, unroll),
        out_shape=[jax.ShapeDtypeStruct((rows, chunk, LANES), jnp.float32)] * space,
        in_specs=[SMEM_SPEC] + [VMEM_SPEC] * 2,
        out_specs=[VMEM_SPEC] * space,
        scratch_shapes=[field] * 7,
        compiler_params=pltpu.CompilerParams(vmem_limit_bytes=VMEM_LIMIT),
        cost_estimate=pl.CostEstimate(
            flops=75 * planes * tiles * SUBLANES * LANES,
            bytes_accessed=2 * planes * tiles * chunk * LANES * 4,
            transcendentals=0,
        ),
        name="filter",
    )(here, x, v)


def pack_kernel(space, band, share, chunk, subs, here_ref, *refs):
    blocks, out = refs[:-1], refs[-1]
    here = here_ref[0]
    for k in range(space):
        group = here - k
        group = jnp.where(group < 0, group + space, group)
        for sub in range(subs):
            first = pl.multiple_of((group * subs + sub) * chunk, chunk)
            block = blocks[k * subs + sub]
            for b in range(band):
                for q in range(share):
                    out[b, pl.ds(first, chunk), q * LANES : (q + 1) * LANES] = block[b * share + q]


def pack(here, blocks, space, band, share, chunk, subs):
    return pl.pallas_call(
        functools.partial(pack_kernel, space, band, share, chunk, subs),
        out_shape=jax.ShapeDtypeStruct((band, space * subs * chunk, share * LANES), jnp.float32),
        in_specs=[SMEM_SPEC] + [VMEM_SPEC] * len(blocks),
        out_specs=VMEM_SPEC,
        compiler_params=pltpu.CompilerParams(vmem_limit_bytes=VMEM_LIMIT),
        cost_estimate=pl.CostEstimate(
            flops=0, bytes_accessed=8 * band * space * subs * chunk * share * LANES, transcendentals=0
        ),
        name="pack",
    )(here, *blocks)


def unpack_kernel(space, rows, chunk, subs_of, here_ref, *refs):
    blocks, out = refs[:-1], refs[-1]
    here = here_ref[0]
    start = 0
    taken = 0
    for subs in subs_of:
        for k in range(space):
            group = here - k
            group = jnp.where(group < 0, group + space, group)
            for sub in range(subs):
                block = blocks[taken + k * subs + sub]
                first = (start + (group * subs + sub) * chunk) * rows
                for row in range(rows):
                    out[pl.ds(first + row, chunk, stride=rows), :] = block[row]
        taken += space * subs
        start += space * subs * chunk


def unpack(here, blocks, space, rows, chunk, subs_of):
    count = sum(subs_of) * space * chunk
    return pl.pallas_call(
        functools.partial(unpack_kernel, space, rows, chunk, subs_of),
        out_shape=jax.ShapeDtypeStruct((count * rows, LANES), jnp.float32),
        in_specs=[SMEM_SPEC] + [VMEM_SPEC] * len(blocks),
        out_specs=VMEM_SPEC,
        compiler_params=pltpu.CompilerParams(vmem_limit_bytes=VMEM_LIMIT),
        cost_estimate=pl.CostEstimate(flops=0, bytes_accessed=8 * count * rows * LANES, transcendentals=0),
        name="unpack",
    )(here, *blocks)


def gram_kernel(band, count, space, chunk, places, which_ref, *refs):
    parts, out, wide = refs[:-2], refs[-2], refs[-1]
    for b in range(band):
        for part, (base, pitch) in zip(parts, places):
            for g in range(space):
                first = b * count + base + g * pitch
                wide[first : first + chunk, :] = part[b, g * chunk : (g + 1) * chunk, :]
    which = which_ref[0]
    pairs = band // 2
    picked = [wide[pl.ds(pl.multiple_of((2 * z + which) * count, SUBLANES), count), :] for z in range(pairs)]
    left = jnp.concatenate(picked, axis=0)
    left_hi = left.astype(jnp.bfloat16)
    left_lo = (left - left_hi.astype(jnp.float32)).astype(jnp.bfloat16)
    total = band * count
    step = 256 if total % 256 == 0 else total

    def dot(a, b):
        return lax.dot_general(a, b, (((1,), (1,)), ((), ())), preferred_element_type=jnp.float32)

    for c in range(0, total, step):
        right = wide[c : c + step, :]
        hi = right.astype(jnp.bfloat16)
        lo = (right - hi.astype(jnp.float32)).astype(jnp.bfloat16)
        out[:, c : c + step] = dot(left_hi, hi) + (dot(left_hi, lo) + dot(left_lo, hi))


def gram(which, parts, space, chunk, places):
    band = parts[0].shape[0]
    count = sum(p.shape[1] for p in parts)
    cells = parts[0].shape[2]
    return pl.pallas_call(
        functools.partial(gram_kernel, band, count, space, chunk, places),
        out_shape=jax.ShapeDtypeStruct((band // 2 * count, band * count), jnp.float32),
        in_specs=[SMEM_SPEC] + [VMEM_SPEC] * len(parts),
        out_specs=VMEM_SPEC,
        scratch_shapes=[pltpu.VMEM((band * count, cells), jnp.float32)],
        compiler_params=pltpu.CompilerParams(vmem_limit_bytes=VMEM_LIMIT),
        cost_estimate=pl.CostEstimate(
            flops=3 * band * band * count * count * cells,
            bytes_accessed=4 * band * count * (cells + band * count // 2),
            transcendentals=0,
        ),
        name="gram",
    )(which, *parts)


def combine_kernel(space, here_ref, a_ref, b_ref, *outs):
    for k, out in enumerate(outs):
        group = here_ref[0] + k
        group = jnp.where(group >= space, group - space, group)
        for z in range(out.shape[0]):
            out[z] = a_ref[z, group] + b_ref[z, group]


def combine(here, a, b):
    pairs, space, own, columns = a.shape
    return pl.pallas_call(
        functools.partial(combine_kernel, space),
        out_shape=[jax.ShapeDtypeStruct((pairs, own, columns), jnp.float32)] * space,
        in_specs=[SMEM_SPEC] + [VMEM_SPEC] * 2,
        out_specs=[VMEM_SPEC] * space,
        compiler_params=pltpu.CompilerParams(vmem_limit_bytes=VMEM_LIMIT),
        cost_estimate=pl.CostEstimate(flops=a.size, bytes_accessed=12 * a.size, transcendentals=0),
        name="combine",
    )(here, a, b)


def place_kernel(space, here_ref, *refs):
    parts, out = refs[:-1], refs[-1]
    for k, part in enumerate(parts):
        group = here_ref[0] - k
        group = jnp.where(group < 0, group + space, group)
        out[group] = part[...]


def place(here, parts):
    space = len(parts)
    own, columns = parts[0].shape
    return pl.pallas_call(
        functools.partial(place_kernel, space),
        out_shape=jax.ShapeDtypeStruct((space, own, columns), jnp.float32),
        in_specs=[SMEM_SPEC] + [VMEM_SPEC] * space,
        out_specs=VMEM_SPEC,
        compiler_params=pltpu.CompilerParams(vmem_limit_bytes=VMEM_LIMIT),
        cost_estimate=pl.CostEstimate(flops=0, bytes_accessed=8 * space * own * columns, transcendentals=0),
        name="place",
    )(here, *parts)


def rotate(x, axis, step):
    size = lax.axis_size(axis)
    return lax.ppermute(x, axis, [(i, (i + step) % size) for i in range(size)])


def shards(orbitals, potential):
    space = lax.axis_size("space")
    band = lax.axis_size("band")
    count, layers, plane = orbitals.shape
    tiles = plane // LANES
    rows = tiles * layers
    share = rows // band
    own = count // space
    chunk = max(c for c in range(1, SUBLANES + 1) if own % c == 0)
    chunks = own // chunk
    groups = [1] if chunks == 1 else [1, chunks - 1]

    s_index = lax.axis_index("space")
    b_index = lax.axis_index("band")
    here = s_index.reshape(1)

    def as_rows(x):
        n = x.shape[0]
        return x.reshape(n, layers, tiles, LANES).transpose(0, 2, 1, 3).reshape(n * rows, LANES)

    def over_space(x):
        return lax.all_to_all(x, "space", split_axis=0, concat_axis=0, tiled=True)

    head = orbitals[: space * chunk].reshape(space, chunk, layers, plane)
    slab_v = jnp.broadcast_to(potential[None, None], (space, 1, layers, plane))
    head = jnp.concatenate([head, slab_v], axis=1).reshape(space * (chunk + 1), layers, plane)
    head = over_space(head)
    arrived = [head]
    if chunks > 1:
        head, tail = lax.optimization_barrier((head, orbitals[space * chunk :]))
        arrived = [head, over_space(tail)]
    arrived = [as_rows(x) for x in arrived]

    all_blocks = []
    parts = []
    places = []
    first = 0
    for subs, x in zip(groups, arrived):
        made = []
        for sub in range(subs):
            outs = run_filter(here, x, arrived[0], sub * chunk, space, layers, tiles, chunk)
            blocks = [outs[0]] + [rotate(outs[k], "space", k) for k in range(1, space)]
            made.append(blocks)
            packed = pack(here, blocks, space, band, share, chunk, 1)
            if parts:
                parts[-1], packed = lax.optimization_barrier((parts[-1], packed))
            parts.append(lax.all_to_all(packed, "band", split_axis=0, concat_axis=0, tiled=True))
            places.append((first + sub * chunk, subs * chunk))
        all_blocks += [made[sub][k] for k in range(space) for sub in range(subs)]
        first += space * subs * chunk

    result = unpack(here, all_blocks, space, rows, chunk, groups)
    parts[-1], result = lax.optimization_barrier((parts[-1], result))
    result = result.reshape(count, tiles, layers, LANES).transpose(0, 2, 1, 3).reshape(count, layers, plane)

    pairs = band // 2
    core = b_index % 2
    pair = b_index // 2

    def half(which):
        return gram(which.reshape(1), parts, space, chunk, places)

    other = lax.ppermute(half(1 - core), "band", [(i, i ^ 1) for i in range(band)])
    split = (pairs, space, own, band * count)
    sums = combine(here, half(core).reshape(split), other.reshape(split))

    mine = sums[0]
    for k in range(1, space):
        mine = mine + rotate(sums[k], "space", k)

    final = lax.dynamic_index_in_dim(mine, pair, 0, keepdims=False)
    for k in range(1, pairs):
        sent = lax.dynamic_index_in_dim(mine, (pair + k) % pairs, 0, keepdims=False)
        final = final + rotate(sent, "band", 2 * k)
    final = final * (1.0 / (layers * space * plane))

    margin = place(here, [final] + [rotate(final, "space", k) for k in range(1, space)])
    return result, margin.reshape(count, band * count)


def solution(mesh):
    return jax.shard_map(
        shards,
        mesh=mesh,
        in_specs=(P("band", "space", None), P("space", None)),
        out_specs=(P("band", "space", None), P("band", None)),
        check_vma=False,
    )
```

```python
import functools

import jax
import jax.numpy as jnp
from jax import lax
from jax.experimental import pallas as pl
from jax.experimental.pallas import tpu as pltpu
from jax.sharding import PartitionSpec as P

NZ = 64
LANES = 128
SUBLANES = 8
VMEM_LIMIT = 40 * 1024 * 1024


def filter_kernel(space, layers, tiles, chunk, pitch, offset, unroll, here_ref, x_ref, *refs):
    v_refs, out_refs = refs[:space], refs[space : 2 * space]
    f0, r0, f1, r1, f2, r2, coef = refs[2 * space :]
    planes = space * layers
    rows = tiles * layers
    lane = lax.broadcasted_iota(jnp.int32, (chunk, LANES), 1)
    depth = lane % NZ
    first_half = lane < NZ
    starts = [depth < 1, depth < 2]
    ends = [depth >= NZ - 1, depth >= NZ - 2]
    here = here_ref[0]

    def load(tile, carry):
        for p in range(planes):
            s, l = divmod(p, layers)
            row = tile * layers + l
            slab = here + s
            slab = jnp.where(slab >= space, slab - space, slab)
            v = x_ref[pl.ds((slab * pitch + offset) * rows + row, chunk, stride=rows), :]
            f0[tile, p] = v
            r0[tile, p] = pltpu.roll(v, NZ, 1)
            w = v_refs[s][pl.ds(row, 1), :]
            coef[tile, p] = jnp.broadcast_to(0.25 * w - 0.5625, (chunk, LANES))
        return carry

    def stencil(f, r, tile):
        up = jnp.where(tile == tiles - 1, 0, tile + 1)
        down = jnp.where(tile == 0, tiles - 1, tile - 1)
        v = [f[tile, p] for p in range(planes)]
        pairs = {}

        def pair(a, b):
            key = (min(a, b), max(a, b))
            if key not in pairs:
                pairs[key] = v[a] + v[b]
            return pairs[key]

        out = []
        for p in range(planes):
            rolled = r[tile, p]
            near = pair((p - 1) % planes, (p + 1) % planes)
            far = pair((p - 2) % planes, (p + 2) % planes)
            far = far + (f[up, p] + f[down, p])
            near = near + (rolled + jnp.where(first_half, r[down, p], r[up, p]))
            near = near + pltpu.roll(jnp.where(starts[0], rolled, v[p]), LANES - 1, 1)
            near = near + pltpu.roll(jnp.where(ends[0], rolled, v[p]), 1, 1)
            far = far + pltpu.roll(jnp.where(starts[1], rolled, v[p]), LANES - 2, 1)
            far = far + pltpu.roll(jnp.where(ends[1], rolled, v[p]), 2, 1)
            out.append((v[p], far - 16.0 * near))
        return out

    def first(tile, carry):
        for p, (v, s) in enumerate(stencil(f0, r0, tile)):
            y = (1.0 / 96.0) * s + coef[tile, p] * v
            f1[tile, p] = y
            r1[tile, p] = pltpu.roll(y, NZ, 1)
        return carry

    def second(tile, carry):
        for p, (v, s) in enumerate(stencil(f1, r1, tile)):
            y = 2.0 * ((1.0 / 96.0) * s + coef[tile, p] * v) - f0[tile, p]
            f2[tile, p] = y
            r2[tile, p] = pltpu.roll(y, NZ, 1)
        return carry

    def third(tile, carry):
        for p, (v, s) in enumerate(stencil(f2, r2, tile)):
            y = 2.0 * ((1.0 / 96.0) * s + coef[tile, p] * v) - f1[tile, p]
            out_refs[p // layers][tile * layers + p % layers] = y
        return carry

    for step in (load, first, second, third):
        lax.fori_loop(0, tiles, step, 0, unroll=unroll)


VMEM_SPEC = pl.BlockSpec(memory_space=pltpu.VMEM)
SMEM_SPEC = pl.BlockSpec(memory_space=pltpu.SMEM)


def run_filter(here, x, vs, offset, space, layers, tiles, chunk):
    rows = tiles * layers
    planes = space * layers
    pitch = x.shape[0] // (space * rows)
    field = pltpu.VMEM((tiles, planes, chunk, LANES), jnp.float32)
    unroll = 8 if tiles % 8 == 0 and planes <= 8 else 1
    return pl.pallas_call(
        functools.partial(filter_kernel, space, layers, tiles, chunk, pitch, offset, unroll),
        out_shape=[jax.ShapeDtypeStruct((rows, chunk, LANES), jnp.float32)] * space,
        in_specs=[SMEM_SPEC] + [VMEM_SPEC] * (1 + space),
        out_specs=[VMEM_SPEC] * space,
        scratch_shapes=[field] * 7,
        compiler_params=pltpu.CompilerParams(vmem_limit_bytes=VMEM_LIMIT),
        cost_estimate=pl.CostEstimate(
            flops=75 * planes * tiles * SUBLANES * LANES,
            bytes_accessed=2 * planes * tiles * chunk * LANES * 4,
            transcendentals=0,
        ),
        name="filter",
    )(here, x, *vs)


def partner(index, size, k, forward=True):
    if size & (size - 1) == 0:
        return index ^ k
    moved = index + k if forward else index - k + size
    return jnp.where(moved >= size, moved - size, moved)


def exchange(x, axis, k, pitch=1):
    size = lax.axis_size(axis) // pitch
    power = size & (size - 1) == 0
    pairs = []
    for i in range(size):
        target = i ^ k if power else (i + k) % size
        pairs += [(i * pitch + low, target * pitch + low) for low in range(pitch)]
    return lax.ppermute(x, axis, pairs)


def pack_kernel(space, band, share, chunk, subs, here_ref, *refs):
    blocks, outs = refs[: space * subs], refs[space * subs :]
    here, mine = here_ref[0], here_ref[1]
    for k in range(space):
        group = here - k
        group = jnp.where(group < 0, group + space, group)
        for sub in range(subs):
            first = pl.multiple_of((group * subs + sub) * chunk, chunk)
            block = blocks[k * subs + sub]
            for step, out in enumerate(outs):
                target = partner(mine, band, step)
                for q in range(share):
                    out[pl.ds(first, chunk), q * LANES : (q + 1) * LANES] = block[target * share + q]


def pack(here, blocks, space, band, share, chunk, subs):
    shape = (space * subs * chunk, share * LANES)
    return pl.pallas_call(
        functools.partial(pack_kernel, space, band, share, chunk, subs),
        out_shape=[jax.ShapeDtypeStruct(shape, jnp.float32)] * band,
        in_specs=[SMEM_SPEC] + [VMEM_SPEC] * len(blocks),
        out_specs=[VMEM_SPEC] * band,
        compiler_params=pltpu.CompilerParams(vmem_limit_bytes=VMEM_LIMIT),
        cost_estimate=pl.CostEstimate(
            flops=0, bytes_accessed=8 * band * space * subs * chunk * share * LANES, transcendentals=0
        ),
        name="pack",
    )(here, *blocks)


def unpack_kernel(space, rows, chunk, subs_of, here_ref, *refs):
    blocks, out = refs[:-1], refs[-1]
    here = here_ref[0]
    start = 0
    taken = 0
    for subs in subs_of:
        for k in range(space):
            group = here - k
            group = jnp.where(group < 0, group + space, group)
            for sub in range(subs):
                block = blocks[taken + k * subs + sub]
                first = (start + (group * subs + sub) * chunk) * rows
                for row in range(rows):
                    out[pl.ds(first + row, chunk, stride=rows), :] = block[row]
        taken += space * subs
        start += space * subs * chunk


def unpack(here, blocks, space, rows, chunk, subs_of):
    count = sum(subs_of) * space * chunk
    return pl.pallas_call(
        functools.partial(unpack_kernel, space, rows, chunk, subs_of),
        out_shape=jax.ShapeDtypeStruct((count * rows, LANES), jnp.float32),
        in_specs=[SMEM_SPEC] + [VMEM_SPEC] * len(blocks),
        out_specs=VMEM_SPEC,
        compiler_params=pltpu.CompilerParams(vmem_limit_bytes=VMEM_LIMIT),
        cost_estimate=pl.CostEstimate(flops=0, bytes_accessed=8 * count * rows * LANES, transcendentals=0),
        name="unpack",
    )(here, *blocks)


def gram_kernel(band, count, space, chunk, places, which_ref, *refs):
    parts, out, wide = list(refs[:-2]), refs[-2], refs[-1]
    own = count // space
    for offset, subs in places:
        size = subs * chunk
        for step in range(band):
            source = partner(which_ref[1], band, step, forward=False)
            part = parts.pop(0)
            for g in range(space):
                first = pl.multiple_of(source * count + g * own + offset, chunk)
                wide[pl.ds(first, size), :] = part[g * size : (g + 1) * size, :]
    which = which_ref[0]
    pairs = band // 2
    picked = [wide[pl.ds(pl.multiple_of((2 * z + which) * count, SUBLANES), count), :] for z in range(pairs)]
    left = jnp.concatenate(picked, axis=0)
    left_hi = left.astype(jnp.bfloat16)
    left_lo = (left - left_hi.astype(jnp.float32)).astype(jnp.bfloat16)
    total = band * count
    step = 256 if total % 256 == 0 else total

    def dot(a, b):
        return lax.dot_general(a, b, (((1,), (1,)), ((), ())), preferred_element_type=jnp.float32)

    for c in range(0, total, step):
        right = wide[c : c + step, :]
        hi = right.astype(jnp.bfloat16)
        lo = (right - hi.astype(jnp.float32)).astype(jnp.bfloat16)
        out[:, c : c + step] = dot(left_hi, hi) + (dot(left_hi, lo) + dot(left_lo, hi))


def gram(which, parts, band, count, space, chunk, places):
    cells = parts[0].shape[-1]
    return pl.pallas_call(
        functools.partial(gram_kernel, band, count, space, chunk, places),
        out_shape=jax.ShapeDtypeStruct((band // 2 * count, band * count), jnp.float32),
        in_specs=[SMEM_SPEC] + [VMEM_SPEC] * len(parts),
        out_specs=VMEM_SPEC,
        scratch_shapes=[pltpu.VMEM((band * count, cells), jnp.float32)],
        compiler_params=pltpu.CompilerParams(vmem_limit_bytes=VMEM_LIMIT),
        cost_estimate=pl.CostEstimate(
            flops=3 * band * band * count * count * cells,
            bytes_accessed=4 * band * count * (cells + band * count // 2),
            transcendentals=0,
        ),
        name="gram",
    )(which, *parts)


def combine_kernel(space, here_ref, a_ref, b_ref, *outs):
    for k, out in enumerate(outs):
        group = here_ref[0] + k
        group = jnp.where(group >= space, group - space, group)
        for z in range(out.shape[0]):
            out[z] = a_ref[z, group] + b_ref[z, group]


def combine(here, a, b):
    pairs, space, own, columns = a.shape
    return pl.pallas_call(
        functools.partial(combine_kernel, space),
        out_shape=[jax.ShapeDtypeStruct((pairs, own, columns), jnp.float32)] * space,
        in_specs=[SMEM_SPEC] + [VMEM_SPEC] * 2,
        out_specs=[VMEM_SPEC] * space,
        compiler_params=pltpu.CompilerParams(vmem_limit_bytes=VMEM_LIMIT),
        cost_estimate=pl.CostEstimate(flops=a.size, bytes_accessed=12 * a.size, transcendentals=0),
        name="combine",
    )(here, a, b)


def place_kernel(space, here_ref, *refs):
    parts, out = refs[:-1], refs[-1]
    for k, part in enumerate(parts):
        group = here_ref[0] - k
        group = jnp.where(group < 0, group + space, group)
        out[group] = part[...]


def place(here, parts):
    space = len(parts)
    own, columns = parts[0].shape
    return pl.pallas_call(
        functools.partial(place_kernel, space),
        out_shape=jax.ShapeDtypeStruct((space, own, columns), jnp.float32),
        in_specs=[SMEM_SPEC] + [VMEM_SPEC] * space,
        out_specs=VMEM_SPEC,
        compiler_params=pltpu.CompilerParams(vmem_limit_bytes=VMEM_LIMIT),
        cost_estimate=pl.CostEstimate(flops=0, bytes_accessed=8 * space * own * columns, transcendentals=0),
        name="place",
    )(here, *parts)


def rotate(x, axis, step):
    size = lax.axis_size(axis)
    return lax.ppermute(x, axis, [(i, (i + step) % size) for i in range(size)])


def shards(orbitals, potential):
    space = lax.axis_size("space")
    band = lax.axis_size("band")
    count, layers, plane = orbitals.shape
    tiles = plane // LANES
    rows = tiles * layers
    share = rows // band
    own = count // space
    chunk = max(c for c in range(1, SUBLANES + 1) if own % c == 0)
    chunks = own // chunk

    s_index = lax.axis_index("space")
    b_index = lax.axis_index("band")
    here = jnp.stack([s_index, b_index])

    def as_rows(x):
        n = x.shape[0]
        return x.reshape(n, layers, tiles, LANES).transpose(0, 2, 1, 3).reshape(n * rows, LANES)

    own_v = as_rows(potential[None])
    vs = [own_v] + [rotate(own_v, "space", space - k) for k in range(1, space)]
    arrived = as_rows(lax.all_to_all(orbitals, "space", split_axis=0, concat_axis=0, tiled=True))

    def filtered(c, x):
        outs = run_filter(here, x, vs, c * chunk, space, layers, tiles, chunk)
        return [outs[0]] + [rotate(outs[k], "space", k) for k in range(1, space)]

    order = sorted(range(1, band), reverse=True)
    made = [filtered(0, arrived)]
    if chunks > 1:
        made.append(filtered(1, arrived))
    parts = []
    places = []
    packed = pack(here, made[0], space, band, share, chunk, 1)
    packed, arrived = lax.optimization_barrier((packed, arrived))
    got = {0: packed[0]}
    for k in order:
        got[k] = exchange(packed[k], "band", k)
    places.append((0, 1))
    for c in range(2, chunks):
        made.append(filtered(c, arrived))
    if chunks > 1:
        late = [made[c][k] for k in range(space) for c in range(1, chunks)]
        packed = pack(here, late, space, band, share, chunk, chunks - 1)
        later = {0: packed[0]}
        for k in order:
            got[k], x = lax.optimization_barrier((got[k], packed[k]))
            later[k] = exchange(x, "band", k)
        places.append((chunk, chunks - 1))
    parts += [got[k] for k in range(band)]
    if chunks > 1:
        parts += [later[k] for k in range(band)]
    blocks = [made[c][k] for k in range(space) for c in range(chunks)]

    result = unpack(here, blocks, space, rows, chunk, [chunks])
    parts[-1], result = lax.optimization_barrier((parts[-1], result))
    result = result.reshape(count, tiles, layers, LANES).transpose(0, 2, 1, 3).reshape(count, layers, plane)

    pairs = band // 2
    core = b_index % 2
    pair = b_index // 2

    def half(which):
        return gram(jnp.stack([which, b_index]), parts, band, count, space, chunk, places)

    other = lax.ppermute(half(1 - core), "band", [(i, i ^ 1) for i in range(band)])
    split = (pairs, space, own, band * count)
    sums = combine(here, half(core).reshape(split), other.reshape(split))

    mine = sums[0]
    for k in range(1, space):
        mine = mine + rotate(sums[k], "space", k)

    final = lax.dynamic_index_in_dim(mine, pair, 0, keepdims=False)
    for k in range(1, pairs):
        sent = lax.dynamic_index_in_dim(mine, partner(pair, pairs, k), 0, keepdims=False)
        final = final + exchange(sent, "band", k, 2)
    final = final * (1.0 / (layers * space * plane))

    margin = place(here, [final] + [rotate(final, "space", k) for k in range(1, space)])
    return result, margin.reshape(count, band * count)


def solution(mesh):
    return jax.shard_map(
        shards,
        mesh=mesh,
        in_specs=(P("band", "space", None), P("space", None)),
        out_specs=(P("band", "space", None), P("band", None)),
        check_vma=False,
    )
```

```python
import functools

import jax
import jax.numpy as jnp
from jax import lax
from jax.experimental import pallas as pl
from jax.experimental.pallas import tpu as pltpu
from jax.sharding import PartitionSpec as P

NZ = 64
LANES = 128
SUBLANES = 8
VMEM_LIMIT = 40 * 1024 * 1024


def filter_kernel(space, layers, tiles, chunk, pitch, offset, unroll, here_ref, x_ref, *refs):
    v_refs, out_refs = refs[:space], refs[space : 2 * space]
    f0, r0, f1, r1, f2, r2, coef = refs[2 * space :]
    planes = space * layers
    rows = tiles * layers
    lane = lax.broadcasted_iota(jnp.int32, (chunk, LANES), 1)
    depth = lane % NZ
    first_half = lane < NZ
    starts = [depth < 1, depth < 2]
    ends = [depth >= NZ - 1, depth >= NZ - 2]
    here = here_ref[0]

    def load(tile, carry):
        for p in range(planes):
            s, l = divmod(p, layers)
            row = tile * layers + l
            slab = here + s
            slab = jnp.where(slab >= space, slab - space, slab)
            v = x_ref[pl.ds((slab * pitch + offset) * rows + row, chunk, stride=rows), :]
            f0[tile, p] = v
            r0[tile, p] = pltpu.roll(v, NZ, 1)
            w = v_refs[s][pl.ds(row, 1), :]
            coef[tile, p] = jnp.broadcast_to(0.25 * w - 0.5625, (chunk, LANES))
        return carry

    def stencil(f, r, tile):
        up = jnp.where(tile == tiles - 1, 0, tile + 1)
        down = jnp.where(tile == 0, tiles - 1, tile - 1)
        v = [f[tile, p] for p in range(planes)]
        pairs = {}

        def pair(a, b):
            key = (min(a, b), max(a, b))
            if key not in pairs:
                pairs[key] = v[a] + v[b]
            return pairs[key]

        out = []
        for p in range(planes):
            rolled = r[tile, p]
            near = pair((p - 1) % planes, (p + 1) % planes)
            far = pair((p - 2) % planes, (p + 2) % planes)
            far = far + (f[up, p] + f[down, p])
            near = near + (rolled + jnp.where(first_half, r[down, p], r[up, p]))
            near = near + pltpu.roll(jnp.where(starts[0], rolled, v[p]), LANES - 1, 1)
            near = near + pltpu.roll(jnp.where(ends[0], rolled, v[p]), 1, 1)
            far = far + pltpu.roll(jnp.where(starts[1], rolled, v[p]), LANES - 2, 1)
            far = far + pltpu.roll(jnp.where(ends[1], rolled, v[p]), 2, 1)
            out.append((v[p], far - 16.0 * near))
        return out

    def first(tile, carry):
        for p, (v, s) in enumerate(stencil(f0, r0, tile)):
            y = (1.0 / 96.0) * s + coef[tile, p] * v
            f1[tile, p] = y
            r1[tile, p] = pltpu.roll(y, NZ, 1)
        return carry

    def second(tile, carry):
        for p, (v, s) in enumerate(stencil(f1, r1, tile)):
            y = 2.0 * ((1.0 / 96.0) * s + coef[tile, p] * v) - f0[tile, p]
            f2[tile, p] = y
            r2[tile, p] = pltpu.roll(y, NZ, 1)
        return carry

    def third(tile, carry):
        for p, (v, s) in enumerate(stencil(f2, r2, tile)):
            y = 2.0 * ((1.0 / 96.0) * s + coef[tile, p] * v) - f1[tile, p]
            out_refs[p // layers][tile * layers + p % layers] = y
        return carry

    for step in (load, first, second, third):
        lax.fori_loop(0, tiles, step, 0, unroll=unroll)


VMEM_SPEC = pl.BlockSpec(memory_space=pltpu.VMEM)
SMEM_SPEC = pl.BlockSpec(memory_space=pltpu.SMEM)


def run_filter(here, x, vs, offset, space, layers, tiles, chunk):
    rows = tiles * layers
    planes = space * layers
    pitch = x.shape[0] // (space * rows)
    field = pltpu.VMEM((tiles, planes, chunk, LANES), jnp.float32)
    unroll = 8 if tiles % 8 == 0 and planes <= 8 else 1
    return pl.pallas_call(
        functools.partial(filter_kernel, space, layers, tiles, chunk, pitch, offset, unroll),
        out_shape=[jax.ShapeDtypeStruct((rows, chunk, LANES), jnp.float32)] * space,
        in_specs=[SMEM_SPEC] + [VMEM_SPEC] * (1 + space),
        out_specs=[VMEM_SPEC] * space,
        scratch_shapes=[field] * 7,
        compiler_params=pltpu.CompilerParams(vmem_limit_bytes=VMEM_LIMIT),
        cost_estimate=pl.CostEstimate(
            flops=75 * planes * tiles * SUBLANES * LANES,
            bytes_accessed=2 * planes * tiles * chunk * LANES * 4,
            transcendentals=0,
        ),
        name="filter",
    )(here, x, *vs)


def partner(index, size, k, forward=True):
    if size & (size - 1) == 0:
        return index ^ k
    moved = index + k if forward else index - k + size
    return jnp.where(moved >= size, moved - size, moved)


def exchange(x, axis, k, pitch=1):
    size = lax.axis_size(axis) // pitch
    power = size & (size - 1) == 0
    pairs = []
    for i in range(size):
        target = i ^ k if power else (i + k) % size
        pairs += [(i * pitch + low, target * pitch + low) for low in range(pitch)]
    return lax.ppermute(x, axis, pairs)


def pack_kernel(space, band, share, chunk, subs, here_ref, *refs):
    blocks, outs = refs[: space * subs], refs[space * subs :]
    here, mine = here_ref[0], here_ref[1]
    for k in range(space):
        group = here - k
        group = jnp.where(group < 0, group + space, group)
        for sub in range(subs):
            first = pl.multiple_of((group * subs + sub) * chunk, chunk)
            block = blocks[k * subs + sub]
            for step in range(band):
                out = outs[0].at[step] if len(outs) == 1 else outs[step]
                target = step if len(outs) == 1 else partner(mine, band, step)
                for q in range(share):
                    out[pl.ds(first, chunk), q * LANES : (q + 1) * LANES] = block[target * share + q]


def pack(here, blocks, space, band, share, chunk, subs, apart):
    shape = (space * subs * chunk, share * LANES)
    out_shape = [jax.ShapeDtypeStruct(shape, jnp.float32)] * band
    if not apart:
        out_shape = [jax.ShapeDtypeStruct((band,) + shape, jnp.float32)]
    return pl.pallas_call(
        functools.partial(pack_kernel, space, band, share, chunk, subs),
        out_shape=out_shape,
        in_specs=[SMEM_SPEC] + [VMEM_SPEC] * len(blocks),
        out_specs=[VMEM_SPEC] * len(out_shape),
        compiler_params=pltpu.CompilerParams(vmem_limit_bytes=VMEM_LIMIT),
        cost_estimate=pl.CostEstimate(
            flops=0, bytes_accessed=8 * band * space * subs * chunk * share * LANES, transcendentals=0
        ),
        name="pack",
    )(here, *blocks)


def unpack_kernel(space, rows, chunk, subs_of, here_ref, *refs):
    blocks, out = refs[:-1], refs[-1]
    here = here_ref[0]
    start = 0
    taken = 0
    for subs in subs_of:
        for k in range(space):
            group = here - k
            group = jnp.where(group < 0, group + space, group)
            for sub in range(subs):
                block = blocks[taken + k * subs + sub]
                first = (start + (group * subs + sub) * chunk) * rows
                for row in range(rows):
                    out[pl.ds(first + row, chunk, stride=rows), :] = block[row]
        taken += space * subs
        start += space * subs * chunk


def unpack(here, blocks, space, rows, chunk, subs_of):
    count = sum(subs_of) * space * chunk
    return pl.pallas_call(
        functools.partial(unpack_kernel, space, rows, chunk, subs_of),
        out_shape=jax.ShapeDtypeStruct((count * rows, LANES), jnp.float32),
        in_specs=[SMEM_SPEC] + [VMEM_SPEC] * len(blocks),
        out_specs=VMEM_SPEC,
        compiler_params=pltpu.CompilerParams(vmem_limit_bytes=VMEM_LIMIT),
        cost_estimate=pl.CostEstimate(flops=0, bytes_accessed=8 * count * rows * LANES, transcendentals=0),
        name="unpack",
    )(here, *blocks)


def gram_kernel(band, count, space, chunk, places, which_ref, *refs):
    parts, out, wide = list(refs[:-2]), refs[-2], refs[-1]
    own = count // space
    for offset, subs, apart in places:
        size = subs * chunk
        taken = [parts.pop(0) for _ in range(band)] if apart else parts.pop(0)
        for step in range(band):
            source = partner(which_ref[1], band, step, forward=False) if apart else step
            for g in range(space):
                first = source * count + g * own + offset
                first = pl.multiple_of(first, chunk) if apart else first
                wide[pl.ds(first, size), :] = taken[step][g * size : (g + 1) * size, :]
    which = which_ref[0]
    pairs = band // 2
    picked = [wide[pl.ds(pl.multiple_of((2 * z + which) * count, SUBLANES), count), :] for z in range(pairs)]
    left = jnp.concatenate(picked, axis=0)
    left_hi = left.astype(jnp.bfloat16)
    left_lo = (left - left_hi.astype(jnp.float32)).astype(jnp.bfloat16)
    total = band * count
    step = 256 if total % 256 == 0 else total

    def dot(a, b):
        return lax.dot_general(a, b, (((1,), (1,)), ((), ())), preferred_element_type=jnp.float32)

    for c in range(0, total, step):
        right = wide[c : c + step, :]
        hi = right.astype(jnp.bfloat16)
        lo = (right - hi.astype(jnp.float32)).astype(jnp.bfloat16)
        out[:, c : c + step] = dot(left_hi, hi) + (dot(left_hi, lo) + dot(left_lo, hi))


def gram(which, parts, band, count, space, chunk, places):
    cells = parts[0].shape[-1]
    return pl.pallas_call(
        functools.partial(gram_kernel, band, count, space, chunk, places),
        out_shape=jax.ShapeDtypeStruct((band // 2 * count, band * count), jnp.float32),
        in_specs=[SMEM_SPEC] + [VMEM_SPEC] * len(parts),
        out_specs=VMEM_SPEC,
        scratch_shapes=[pltpu.VMEM((band * count, cells), jnp.float32)],
        compiler_params=pltpu.CompilerParams(vmem_limit_bytes=VMEM_LIMIT),
        cost_estimate=pl.CostEstimate(
            flops=3 * band * band * count * count * cells,
            bytes_accessed=4 * band * count * (cells + band * count // 2),
            transcendentals=0,
        ),
        name="gram",
    )(which, *parts)


def combine_kernel(a_ref, b_ref, out_ref):
    for z in range(a_ref.shape[0]):
        for g in range(a_ref.shape[1]):
            out_ref[g, z] = a_ref[z, g] + b_ref[z, g]


def combine(a, b):
    pairs, space, own, columns = a.shape
    return pl.pallas_call(
        combine_kernel,
        out_shape=jax.ShapeDtypeStruct((space, pairs, own, columns), jnp.float32),
        in_specs=[VMEM_SPEC] * 2,
        out_specs=VMEM_SPEC,
        compiler_params=pltpu.CompilerParams(vmem_limit_bytes=VMEM_LIMIT),
        cost_estimate=pl.CostEstimate(flops=a.size, bytes_accessed=12 * a.size, transcendentals=0),
        name="combine",
    )(a, b)


def rotate(x, axis, step):
    size = lax.axis_size(axis)
    return lax.ppermute(x, axis, [(i, (i + step) % size) for i in range(size)])


def shards(orbitals, potential):
    space = lax.axis_size("space")
    band = lax.axis_size("band")
    count, layers, plane = orbitals.shape
    tiles = plane // LANES
    rows = tiles * layers
    share = rows // band
    own = count // space
    chunk = max(c for c in range(1, SUBLANES + 1) if own % c == 0)
    chunks = own // chunk

    s_index = lax.axis_index("space")
    b_index = lax.axis_index("band")
    here = jnp.stack([s_index, b_index])

    def as_rows(x):
        n = x.shape[0]
        return x.reshape(n, layers, tiles, LANES).transpose(0, 2, 1, 3).reshape(n * rows, LANES)

    own_v = as_rows(potential[None])
    vs = [own_v] + [rotate(own_v, "space", space - k) for k in range(1, space)]
    arrived = as_rows(lax.all_to_all(orbitals, "space", split_axis=0, concat_axis=0, tiled=True))

    def filtered(c, x):
        outs = run_filter(here, x, vs, c * chunk, space, layers, tiles, chunk)
        return [outs[0]] + [rotate(outs[k], "space", k) for k in range(1, space)]

    made = [filtered(c, arrived) for c in range(min(chunks, 2))]
    head = pack(here, made[0], space, band, share, chunk, 1, False)[0]
    head, arrived = lax.optimization_barrier((head, arrived))
    parts = [lax.all_to_all(head, "band", split_axis=0, concat_axis=0, tiled=True)]
    places = [(0, 1, False)]
    made += [filtered(c, arrived) for c in range(2, chunks)]
    if chunks > 1:
        late = [made[c][k] for k in range(space) for c in range(1, chunks)]
        packed = pack(here, late, space, band, share, chunk, chunks - 1, True)
        got = {0: packed[0]}
        for k in reversed(range(1, band)):
            got[k] = exchange(packed[k], "band", k)
        parts += [got[k] for k in range(band)]
        places.append((chunk, chunks - 1, True))
    blocks = [made[c][k] for k in range(space) for c in range(chunks)]

    result = unpack(here, blocks, space, rows, chunk, [chunks])
    parts[-1], result = lax.optimization_barrier((parts[-1], result))
    result = result.reshape(count, tiles, layers, LANES).transpose(0, 2, 1, 3).reshape(count, layers, plane)

    pairs = band // 2
    core = b_index % 2

    def half(which):
        return gram(jnp.stack([which, b_index]), parts, band, count, space, chunk, places)

    other = lax.ppermute(half(1 - core), "band", [(i, i ^ 1) for i in range(band)])
    split = (pairs, space, own, band * count)
    sums = combine(half(core).reshape(split), other.reshape(split))

    def swap(x, axis, groups=None):
        return lax.all_to_all(x, axis, split_axis=0, concat_axis=0, tiled=True, axis_index_groups=groups)

    over_space = jnp.sum(swap(sums, "space"), axis=0)
    same_core = [list(range(low, band, 2)) for low in range(2)]
    final = jnp.sum(swap(over_space, "band", same_core), axis=0) * (1.0 / (layers * space * plane))
    margin = swap(jnp.broadcast_to(final[None], (space, own, band * count)), "space")
    return result, margin.reshape(count, band * count)


def solution(mesh):
    return jax.shard_map(
        shards,
        mesh=mesh,
        in_specs=(P("band", "space", None), P("space", None)),
        out_specs=(P("band", "space", None), P("band", None)),
        check_vma=False,
    )
```

```python
import functools

import jax
import jax.numpy as jnp
import ml_dtypes
import numpy as np
from jax import lax
from jax.experimental import pallas as pl
from jax.experimental.pallas import tpu as pltpu
from jax.sharding import PartitionSpec as P

NZ = 64
LANES = 128
SUBLANES = 8
VMEM_LIMIT = 40 * 1024 * 1024


def plane_matrix():
    wide = 2 * LANES
    matrix = np.zeros((2 * wide, wide), np.float32)
    for y in range(wide // NZ):
        for z in range(NZ):
            column = y * NZ + z
            for step, weight in ((1, -16.0), (-1, -16.0), (2, 1.0), (-2, 1.0)):
                matrix[y * NZ + (z + step) % NZ, column] += weight
                row = y + step
                if row < 0:
                    row += 6
                elif row >= 4:
                    row += 2
                matrix[row * NZ + z, column] += weight
    return matrix.astype(ml_dtypes.bfloat16)


def filter_kernel(space, layers, tiles, chunk, pitch, offset, here_ref, x_ref, m_ref, *refs):
    v_refs, out_refs = refs[:space], refs[space : 2 * space]
    f0, f1, coef, mm, hi, lo = refs[2 * space :]
    planes = space * layers
    rows = tiles * layers
    quads, height, wide = f0.shape
    here = here_ref[0]

    def put(f, j, v):
        f[j] = v
        top = v.astype(jnp.bfloat16)
        hi[j] = top
        lo[j] = (v - top.astype(jnp.float32)).astype(jnp.bfloat16)

    for j in range(quads):
        columns = []
        for half in range(2):
            column = []
            for p in range(planes):
                s, l = divmod(p, layers)
                row = (2 * j + half) * layers + l
                slab = here + s
                slab = jnp.where(slab >= space, slab - space, slab)
                column.append(x_ref[pl.ds((slab * pitch + offset) * rows + row, chunk, stride=rows), :])
                w = v_refs[s][row : row + 1, :]
                coef[j, p * chunk : (p + 1) * chunk, half * LANES : (half + 1) * LANES] = jnp.broadcast_to(
                    0.5 * w - 1.125, (chunk, LANES)
                )
            columns.append(jnp.concatenate(column, axis=0))
        put(f0, j, jnp.concatenate(columns, axis=1))

    def beside(a):
        before = jnp.concatenate([a[quads - 1 :], a[: quads - 1]], axis=0)
        after = jnp.concatenate([a[1:], a[:1]], axis=0)
        return jnp.concatenate([before[:, :, LANES:], after[:, :, :LANES]], axis=2)

    def product():
        top, rest = hi[...], lo[...]
        left = jnp.concatenate([top, beside(top), rest, beside(rest)], axis=2).reshape(quads * height, 4 * wide)
        right = jnp.concatenate([m_ref[...], m_ref[...]], axis=0)
        got = lax.dot_general(left, right, (((1,), (0,)), ((), ())), preferred_element_type=jnp.float32)
        mm[...] = got.reshape(quads, height, wide)

    def stencil(f, j):
        v = f[j]

        def moved(k):
            k = k % planes * chunk
            return jnp.concatenate([v[k:], v[:k]], axis=0) if k else v

        return v, (mm[j] + (moved(2) + moved(-2))) - 16.0 * (moved(1) + moved(-1))

    product()
    for j in range(quads):
        v, s = stencil(f0, j)
        put(f1, j, (1.0 / 96.0) * s + 0.5 * (coef[j] * v))
    product()
    for j in range(quads):
        v, s = stencil(f1, j)
        put(f0, j, ((1.0 / 48.0) * s + coef[j] * v) - f0[j])
    product()
    for j in range(quads):
        v, s = stencil(f0, j)
        y = ((1.0 / 48.0) * s + coef[j] * v) - f1[j]
        for p in range(planes):
            for half in range(2):
                block = y[p * chunk : (p + 1) * chunk, half * LANES : (half + 1) * LANES]
                out_refs[p // layers][(2 * j + half) * layers + p % layers] = block


VMEM_SPEC = pl.BlockSpec(memory_space=pltpu.VMEM)
SMEM_SPEC = pl.BlockSpec(memory_space=pltpu.SMEM)


def run_filter(here, x, matrix, vs, offset, space, layers, tiles, chunk):
    rows = tiles * layers
    planes = space * layers
    pitch = x.shape[0] // (space * rows)
    shape = (tiles // 2, planes * chunk, 2 * LANES)
    return pl.pallas_call(
        functools.partial(filter_kernel, space, layers, tiles, chunk, pitch, offset),
        out_shape=[jax.ShapeDtypeStruct((rows, chunk, LANES), jnp.float32)] * space,
        in_specs=[SMEM_SPEC] + [VMEM_SPEC] * (2 + space),
        out_specs=[VMEM_SPEC] * space,
        scratch_shapes=[pltpu.VMEM(shape, jnp.float32)] * 4 + [pltpu.VMEM(shape, jnp.bfloat16)] * 2,
        compiler_params=pltpu.CompilerParams(vmem_limit_bytes=VMEM_LIMIT),
        cost_estimate=pl.CostEstimate(
            flops=50 * planes * tiles * SUBLANES * LANES,
            bytes_accessed=2 * planes * tiles * chunk * LANES * 4,
            transcendentals=0,
        ),
        name="filter",
    )(here, x, matrix, *vs)


def partner(index, size, k, forward=True):
    if size & (size - 1) == 0:
        return index ^ k
    moved = index + k if forward else index - k + size
    return jnp.where(moved >= size, moved - size, moved)


def exchange(x, axis, k, pitch=1):
    size = lax.axis_size(axis) // pitch
    power = size & (size - 1) == 0
    pairs = []
    for i in range(size):
        target = i ^ k if power else (i + k) % size
        pairs += [(i * pitch + low, target * pitch + low) for low in range(pitch)]
    return lax.ppermute(x, axis, pairs)


def pack_kernel(space, band, share, chunk, subs, here_ref, *refs):
    blocks, outs = refs[: space * subs], refs[space * subs :]
    here, mine = here_ref[0], here_ref[1]
    for k in range(space):
        group = here - k
        group = jnp.where(group < 0, group + space, group)
        for sub in range(subs):
            first = pl.multiple_of((group * subs + sub) * chunk, chunk)
            block = blocks[k * subs + sub]
            for step in range(band):
                out = outs[0].at[step] if len(outs) == 1 else outs[step]
                target = step if len(outs) == 1 else partner(mine, band, step)
                for q in range(share):
                    out[pl.ds(first, chunk), q * LANES : (q + 1) * LANES] = block[target * share + q]


def pack(here, blocks, space, band, share, chunk, subs, apart):
    shape = (space * subs * chunk, share * LANES)
    out_shape = [jax.ShapeDtypeStruct(shape, jnp.float32)] * band
    if not apart:
        out_shape = [jax.ShapeDtypeStruct((band,) + shape, jnp.float32)]
    return pl.pallas_call(
        functools.partial(pack_kernel, space, band, share, chunk, subs),
        out_shape=out_shape,
        in_specs=[SMEM_SPEC] + [VMEM_SPEC] * len(blocks),
        out_specs=[VMEM_SPEC] * len(out_shape),
        compiler_params=pltpu.CompilerParams(vmem_limit_bytes=VMEM_LIMIT),
        cost_estimate=pl.CostEstimate(
            flops=0, bytes_accessed=8 * band * space * subs * chunk * share * LANES, transcendentals=0
        ),
        name="pack",
    )(here, *blocks)


def unpack_kernel(space, rows, chunk, subs_of, here_ref, *refs):
    blocks, out = refs[:-1], refs[-1]
    here = here_ref[0]
    start = 0
    taken = 0
    for subs in subs_of:
        for k in range(space):
            group = here - k
            group = jnp.where(group < 0, group + space, group)
            for sub in range(subs):
                block = blocks[taken + k * subs + sub]
                first = (start + (group * subs + sub) * chunk) * rows
                for row in range(rows):
                    out[pl.ds(first + row, chunk, stride=rows), :] = block[row]
        taken += space * subs
        start += space * subs * chunk


def unpack(here, blocks, space, rows, chunk, subs_of):
    count = sum(subs_of) * space * chunk
    return pl.pallas_call(
        functools.partial(unpack_kernel, space, rows, chunk, subs_of),
        out_shape=jax.ShapeDtypeStruct((count * rows, LANES), jnp.float32),
        in_specs=[SMEM_SPEC] + [VMEM_SPEC] * len(blocks),
        out_specs=VMEM_SPEC,
        compiler_params=pltpu.CompilerParams(vmem_limit_bytes=VMEM_LIMIT),
        cost_estimate=pl.CostEstimate(flops=0, bytes_accessed=8 * count * rows * LANES, transcendentals=0),
        name="unpack",
    )(here, *blocks)


def gram_kernel(band, count, space, chunk, places, which_ref, *refs):
    parts, out, wide = list(refs[:-2]), refs[-2], refs[-1]
    own = count // space
    for offset, subs, apart in places:
        size = subs * chunk
        taken = [parts.pop(0) for _ in range(band)] if apart else parts.pop(0)
        for step in range(band):
            source = partner(which_ref[1], band, step, forward=False) if apart else step
            for g in range(space):
                first = source * count + g * own + offset
                first = pl.multiple_of(first, chunk) if apart else first
                wide[pl.ds(first, size), :] = taken[step][g * size : (g + 1) * size, :]
    which = which_ref[0]
    pairs = band // 2
    picked = [wide[pl.ds(pl.multiple_of((2 * z + which) * count, SUBLANES), count), :] for z in range(pairs)]
    left = jnp.concatenate(picked, axis=0)
    left_hi = left.astype(jnp.bfloat16)
    left_lo = (left - left_hi.astype(jnp.float32)).astype(jnp.bfloat16)
    total = band * count
    step = 256 if total % 256 == 0 else total

    def dot(a, b):
        return lax.dot_general(a, b, (((1,), (1,)), ((), ())), preferred_element_type=jnp.float32)

    for c in range(0, total, step):
        right = wide[c : c + step, :]
        hi = right.astype(jnp.bfloat16)
        lo = (right - hi.astype(jnp.float32)).astype(jnp.bfloat16)
        out[:, c : c + step] = dot(left_hi, hi) + (dot(left_hi, lo) + dot(left_lo, hi))


def gram(which, parts, band, count, space, chunk, places):
    cells = parts[0].shape[-1]
    return pl.pallas_call(
        functools.partial(gram_kernel, band, count, space, chunk, places),
        out_shape=jax.ShapeDtypeStruct((band // 2 * count, band * count), jnp.float32),
        in_specs=[SMEM_SPEC] + [VMEM_SPEC] * len(parts),
        out_specs=VMEM_SPEC,
        scratch_shapes=[pltpu.VMEM((band * count, cells), jnp.float32)],
        compiler_params=pltpu.CompilerParams(vmem_limit_bytes=VMEM_LIMIT),
        cost_estimate=pl.CostEstimate(
            flops=3 * band * band * count * count * cells,
            bytes_accessed=4 * band * count * (cells + band * count // 2),
            transcendentals=0,
        ),
        name="gram",
    )(which, *parts)


def combine_kernel(space, here_ref, a_ref, b_ref, *outs):
    for k, out in enumerate(outs):
        group = here_ref[0] + k
        group = jnp.where(group >= space, group - space, group)
        for z in range(out.shape[0]):
            out[z] = a_ref[z, group] + b_ref[z, group]


def combine(here, a, b):
    pairs, space, own, columns = a.shape
    return pl.pallas_call(
        functools.partial(combine_kernel, space),
        out_shape=[jax.ShapeDtypeStruct((pairs, own, columns), jnp.float32)] * space,
        in_specs=[SMEM_SPEC] + [VMEM_SPEC] * 2,
        out_specs=[VMEM_SPEC] * space,
        compiler_params=pltpu.CompilerParams(vmem_limit_bytes=VMEM_LIMIT),
        cost_estimate=pl.CostEstimate(flops=a.size, bytes_accessed=12 * a.size, transcendentals=0),
        name="combine",
    )(here, a, b)


def place_kernel(space, here_ref, *refs):
    parts, out = refs[:-1], refs[-1]
    for k, part in enumerate(parts):
        group = here_ref[0] - k
        group = jnp.where(group < 0, group + space, group)
        out[group] = part[...]


def place(here, parts):
    space = len(parts)
    own, columns = parts[0].shape
    return pl.pallas_call(
        functools.partial(place_kernel, space),
        out_shape=jax.ShapeDtypeStruct((space, own, columns), jnp.float32),
        in_specs=[SMEM_SPEC] + [VMEM_SPEC] * space,
        out_specs=VMEM_SPEC,
        compiler_params=pltpu.CompilerParams(vmem_limit_bytes=VMEM_LIMIT),
        cost_estimate=pl.CostEstimate(flops=0, bytes_accessed=8 * space * own * columns, transcendentals=0),
        name="place",
    )(here, *parts)


def rotate(x, axis, step):
    size = lax.axis_size(axis)
    return lax.ppermute(x, axis, [(i, (i + step) % size) for i in range(size)])


def shards(orbitals, potential):
    space = lax.axis_size("space")
    band = lax.axis_size("band")
    count, layers, plane = orbitals.shape
    tiles = plane // LANES
    rows = tiles * layers
    share = rows // band
    own = count // space
    chunk = max(c for c in range(1, SUBLANES + 1) if own % c == 0)
    chunks = own // chunk

    s_index = lax.axis_index("space")
    b_index = lax.axis_index("band")
    here = jnp.stack([s_index, b_index])

    def as_rows(x):
        n = x.shape[0]
        return x.reshape(n, layers, tiles, LANES).transpose(0, 2, 1, 3).reshape(n * rows, LANES)

    matrix = jnp.asarray(plane_matrix())
    own_v = as_rows(potential[None])
    vs = [own_v] + [rotate(own_v, "space", space - k) for k in range(1, space)]
    arrived = as_rows(lax.all_to_all(orbitals, "space", split_axis=0, concat_axis=0, tiled=True))

    def filtered(c, x):
        outs = run_filter(here, x, matrix, vs, c * chunk, space, layers, tiles, chunk)
        return [outs[0]] + [rotate(outs[k], "space", k) for k in range(1, space)]

    made = [filtered(c, arrived) for c in range(min(chunks, 2))]
    head = pack(here, made[0], space, band, share, chunk, 1, False)[0]
    head, arrived = lax.optimization_barrier((head, arrived))
    parts = [lax.all_to_all(head, "band", split_axis=0, concat_axis=0, tiled=True)]
    places = [(0, 1, False)]
    made += [filtered(c, arrived) for c in range(2, chunks)]
    if chunks > 1:
        late = [made[c][k] for k in range(space) for c in range(1, chunks)]
        packed = pack(here, late, space, band, share, chunk, chunks - 1, True)
        got = {0: packed[0]}
        for k in reversed(range(1, band)):
            got[k] = exchange(packed[k], "band", k)
        parts += [got[k] for k in range(band)]
        places.append((chunk, chunks - 1, True))
    blocks = [made[c][k] for k in range(space) for c in range(chunks)]

    result = unpack(here, blocks, space, rows, chunk, [chunks])
    parts[-1], result = lax.optimization_barrier((parts[-1], result))
    result = result.reshape(count, tiles, layers, LANES).transpose(0, 2, 1, 3).reshape(count, layers, plane)

    pairs = band // 2
    core = b_index % 2
    pair = b_index // 2

    def half(which):
        return gram(jnp.stack([which, b_index]), parts, band, count, space, chunk, places)

    other = lax.ppermute(half(1 - core), "band", [(i, i ^ 1) for i in range(band)])
    split = (pairs, space, own, band * count)
    sums = combine(here, half(core).reshape(split), other.reshape(split))

    mine = sums[0]
    for k in range(1, space):
        mine = mine + rotate(sums[k], "space", k)

    final = lax.dynamic_index_in_dim(mine, pair, 0, keepdims=False)
    for k in range(1, pairs):
        sent = lax.dynamic_index_in_dim(mine, partner(pair, pairs, k), 0, keepdims=False)
        final = final + exchange(sent, "band", k, 2)
    final = final * (1.0 / (layers * space * plane))

    margin = place(here, [final] + [rotate(final, "space", k) for k in range(1, space)])
    return result, margin.reshape(count, band * count)


def solution(mesh):
    return jax.shard_map(
        shards,
        mesh=mesh,
        in_specs=(P("band", "space", None), P("space", None)),
        out_specs=(P("band", "space", None), P("band", None)),
        check_vma=False,
    )
```

```python
import functools

import jax
import jax.numpy as jnp
import ml_dtypes
import numpy as np
from jax import lax
from jax.experimental import pallas as pl
from jax.experimental.pallas import tpu as pltpu
from jax.sharding import PartitionSpec as P

NZ = 64
LANES = 128
SUBLANES = 8
VMEM_LIMIT = 12 * 1024 * 1024


def plane_matrix():
    wide = 2 * LANES
    matrix = np.zeros((2 * wide, wide), np.float32)
    for y in range(wide // NZ):
        for z in range(NZ):
            column = y * NZ + z
            for step, weight in ((1, -16.0), (-1, -16.0), (2, 1.0), (-2, 1.0)):
                matrix[y * NZ + (z + step) % NZ, column] += weight
                row = y + step
                if row < 0:
                    row += 6
                elif row >= 4:
                    row += 2
                matrix[row * NZ + z, column] += weight
    return matrix.astype(ml_dtypes.bfloat16)


def filter_kernel(space, layers, tiles, chunk, pitch, offset, here_ref, x_ref, m_ref, *refs):
    v_refs, out_refs = refs[:space], refs[space : 2 * space]
    f0, f1, coef, mm, hi, lo = refs[2 * space :]
    planes = space * layers
    rows = tiles * layers
    quads, height, wide = f0.shape
    here = here_ref[0]

    def put(f, j, v):
        f[j] = v
        top = v.astype(jnp.bfloat16)
        hi[j] = top
        lo[j] = (v - top.astype(jnp.float32)).astype(jnp.bfloat16)

    for j in range(quads):
        columns = []
        for half in range(2):
            column = []
            for p in range(planes):
                s, l = divmod(p, layers)
                row = (2 * j + half) * layers + l
                slab = here + s
                slab = jnp.where(slab >= space, slab - space, slab)
                column.append(x_ref[pl.ds((slab * pitch + offset) * rows + row, chunk, stride=rows), :])
                w = v_refs[s][row : row + 1, :]
                coef[j, p * chunk : (p + 1) * chunk, half * LANES : (half + 1) * LANES] = jnp.broadcast_to(
                    0.5 * w - 1.125, (chunk, LANES)
                )
            columns.append(jnp.concatenate(column, axis=0))
        put(f0, j, jnp.concatenate(columns, axis=1))

    def beside(a):
        before = jnp.concatenate([a[quads - 1 :], a[: quads - 1]], axis=0)
        after = jnp.concatenate([a[1:], a[:1]], axis=0)
        return jnp.concatenate([before[:, :, LANES:], after[:, :, :LANES]], axis=2)

    def product():
        top, rest = hi[...], lo[...]
        left = jnp.concatenate([top, beside(top), rest, beside(rest)], axis=2).reshape(quads * height, 4 * wide)
        right = jnp.concatenate([m_ref[...], m_ref[...]], axis=0)
        got = lax.dot_general(left, right, (((1,), (0,)), ((), ())), preferred_element_type=jnp.float32)
        mm[...] = got.reshape(quads, height, wide)

    def stencil(f, j):
        v = f[j]

        def moved(k):
            k = k % planes * chunk
            return jnp.concatenate([v[k:], v[:k]], axis=0) if k else v

        return v, (mm[j] + (moved(2) + moved(-2))) - 16.0 * (moved(1) + moved(-1))

    product()
    for j in range(quads):
        v, s = stencil(f0, j)
        put(f1, j, (1.0 / 96.0) * s + 0.5 * (coef[j] * v))
    product()
    for j in range(quads):
        v, s = stencil(f1, j)
        put(f0, j, ((1.0 / 48.0) * s + coef[j] * v) - f0[j])
    product()
    for j in range(quads):
        v, s = stencil(f0, j)
        y = ((1.0 / 48.0) * s + coef[j] * v) - f1[j]
        for p in range(planes):
            for half in range(2):
                block = y[p * chunk : (p + 1) * chunk, half * LANES : (half + 1) * LANES]
                out_refs[p // layers][(2 * j + half) * layers + p % layers] = block


VMEM_SPEC = pl.BlockSpec(memory_space=pltpu.VMEM)
SMEM_SPEC = pl.BlockSpec(memory_space=pltpu.SMEM)


def run_filter(here, x, matrix, vs, offset, space, layers, tiles, chunk):
    rows = tiles * layers
    planes = space * layers
    pitch = x.shape[0] // (space * rows)
    shape = (tiles // 2, planes * chunk, 2 * LANES)
    return pl.pallas_call(
        functools.partial(filter_kernel, space, layers, tiles, chunk, pitch, offset),
        out_shape=[jax.ShapeDtypeStruct((rows, chunk, LANES), jnp.float32)] * space,
        in_specs=[SMEM_SPEC] + [VMEM_SPEC] * (2 + space),
        out_specs=[VMEM_SPEC] * space,
        scratch_shapes=[pltpu.VMEM(shape, jnp.float32)] * 4 + [pltpu.VMEM(shape, jnp.bfloat16)] * 2,
        compiler_params=pltpu.CompilerParams(vmem_limit_bytes=VMEM_LIMIT),
        cost_estimate=pl.CostEstimate(
            flops=50 * planes * tiles * SUBLANES * LANES,
            bytes_accessed=2 * planes * tiles * chunk * LANES * 4,
            transcendentals=0,
        ),
        name="filter",
    )(here, x, matrix, *vs)


def partner(index, size, k, forward=True):
    if size & (size - 1) == 0:
        return index ^ k
    moved = index + k if forward else index - k + size
    return jnp.where(moved >= size, moved - size, moved)


def exchange(x, axis, k, pitch=1):
    size = lax.axis_size(axis) // pitch
    power = size & (size - 1) == 0
    pairs = []
    for i in range(size):
        target = i ^ k if power else (i + k) % size
        pairs += [(i * pitch + low, target * pitch + low) for low in range(pitch)]
    return lax.ppermute(x, axis, pairs)


def pack_kernel(space, band, share, chunk, subs, here_ref, *refs):
    blocks, outs = refs[: space * subs], refs[space * subs :]
    here, mine = here_ref[0], here_ref[1]
    for k in range(space):
        group = here - k
        group = jnp.where(group < 0, group + space, group)
        for sub in range(subs):
            first = pl.multiple_of((group * subs + sub) * chunk, chunk)
            block = blocks[k * subs + sub]
            for step in range(band):
                out = outs[0].at[step] if len(outs) == 1 else outs[step]
                target = step if len(outs) == 1 else partner(mine, band, step)
                for q in range(share):
                    out[pl.ds(first, chunk), q * LANES : (q + 1) * LANES] = block[target * share + q]


def pack(here, blocks, space, band, share, chunk, subs, apart):
    shape = (space * subs * chunk, share * LANES)
    out_shape = [jax.ShapeDtypeStruct(shape, jnp.float32)] * band
    if not apart:
        out_shape = [jax.ShapeDtypeStruct((band,) + shape, jnp.float32)]
    return pl.pallas_call(
        functools.partial(pack_kernel, space, band, share, chunk, subs),
        out_shape=out_shape,
        in_specs=[SMEM_SPEC] + [VMEM_SPEC] * len(blocks),
        out_specs=[VMEM_SPEC] * len(out_shape),
        compiler_params=pltpu.CompilerParams(vmem_limit_bytes=VMEM_LIMIT),
        cost_estimate=pl.CostEstimate(
            flops=0, bytes_accessed=8 * band * space * subs * chunk * share * LANES, transcendentals=0
        ),
        name="pack",
    )(here, *blocks)


def unpack_kernel(space, rows, chunk, subs_of, here_ref, *refs):
    blocks, out = refs[:-1], refs[-1]
    here = here_ref[0]
    start = 0
    taken = 0
    for subs in subs_of:
        for k in range(space):
            group = here - k
            group = jnp.where(group < 0, group + space, group)
            for sub in range(subs):
                block = blocks[taken + k * subs + sub]
                first = (start + (group * subs + sub) * chunk) * rows
                for row in range(rows):
                    out[pl.ds(first + row, chunk, stride=rows), :] = block[row]
        taken += space * subs
        start += space * subs * chunk


def unpack(here, blocks, space, rows, chunk, subs_of):
    count = sum(subs_of) * space * chunk
    return pl.pallas_call(
        functools.partial(unpack_kernel, space, rows, chunk, subs_of),
        out_shape=jax.ShapeDtypeStruct((count * rows, LANES), jnp.float32),
        in_specs=[SMEM_SPEC] + [VMEM_SPEC] * len(blocks),
        out_specs=VMEM_SPEC,
        compiler_params=pltpu.CompilerParams(vmem_limit_bytes=VMEM_LIMIT),
        cost_estimate=pl.CostEstimate(flops=0, bytes_accessed=8 * count * rows * LANES, transcendentals=0),
        name="unpack",
    )(here, *blocks)


def half_product(band, count, which, hi, lo, out):
    def picked(x):
        return jnp.concatenate([x[2 * z + which] for z in range(band // 2)], axis=0)

    def dot(a, b):
        return lax.dot_general(a, b, (((1,), (1,)), ((), ())), preferred_element_type=jnp.float32)

    left_hi, left_lo = picked(hi), picked(lo)
    per_step = max(n for n in range(1, band + 1) if band % n == 0 and n * count <= 384)
    for b in range(0, band, per_step):
        right_hi = jnp.concatenate([hi[b + n] for n in range(per_step)], axis=0)
        right_lo = jnp.concatenate([lo[b + n] for n in range(per_step)], axis=0)
        columns = slice(b * count, (b + per_step) * count)
        out[:, columns] = dot(left_hi, right_hi) + (dot(left_hi, right_lo) + dot(left_lo, right_hi))


def gram_kernel(band, count, space, chunk, places, which_ref, *refs):
    parts, (out, hi, lo, wide) = list(refs[:-4]), refs[-4:]
    own = count // space
    for offset, subs, apart in places:
        size = subs * chunk
        taken = [parts.pop(0) for _ in range(band)] if apart else parts.pop(0)
        for step in range(band):
            source = partner(which_ref[1], band, step, forward=False) if apart else step
            for g in range(space):
                wide[source, g * own + offset : g * own + offset + size, :] = taken[step][g * size : (g + 1) * size, :]
    for b in range(band):
        top = wide[b].astype(jnp.bfloat16)
        hi[b] = top
        lo[b] = (wide[b] - top.astype(jnp.float32)).astype(jnp.bfloat16)
    half_product(band, count, 1 - which_ref[0], hi, lo, out)


def own_gram_kernel(band, count, which_ref, hi, lo, out):
    half_product(band, count, which_ref[0], hi, lo, out)


def gram(which, parts, band, count, space, chunk, places):
    cells = parts[0].shape[-1]
    half = jax.ShapeDtypeStruct((band // 2 * count, band * count), jnp.float32)
    narrow = jax.ShapeDtypeStruct((band, count, cells), jnp.bfloat16)
    params = pltpu.CompilerParams(vmem_limit_bytes=VMEM_LIMIT)
    cost = pl.CostEstimate(
        flops=3 * band * band * count * count * cells,
        bytes_accessed=4 * band * count * (cells + band * count // 2),
        transcendentals=0,
    )
    other, hi, lo = pl.pallas_call(
        functools.partial(gram_kernel, band, count, space, chunk, places),
        out_shape=[half, narrow, narrow],
        in_specs=[SMEM_SPEC] + [VMEM_SPEC] * len(parts),
        out_specs=[VMEM_SPEC] * 3,
        scratch_shapes=[pltpu.VMEM((band, count, cells), jnp.float32)],
        compiler_params=params,
        cost_estimate=cost,
        name="gram",
    )(which, *parts)
    own = pl.pallas_call(
        functools.partial(own_gram_kernel, band, count),
        out_shape=half,
        in_specs=[SMEM_SPEC] + [VMEM_SPEC] * 2,
        out_specs=VMEM_SPEC,
        compiler_params=params,
        cost_estimate=cost,
        name="own_gram",
    )(which, hi, lo)
    return own, other


def combine_kernel(space, here_ref, a_ref, b_ref, *outs):
    for k, out in enumerate(outs):
        group = here_ref[0] + k
        group = jnp.where(group >= space, group - space, group)
        for z in range(out.shape[0]):
            out[z] = a_ref[z, group] + b_ref[z, group]


def combine(here, a, b):
    pairs, space, own, columns = a.shape
    return pl.pallas_call(
        functools.partial(combine_kernel, space),
        out_shape=[jax.ShapeDtypeStruct((pairs, own, columns), jnp.float32)] * space,
        in_specs=[SMEM_SPEC] + [VMEM_SPEC] * 2,
        out_specs=[VMEM_SPEC] * space,
        compiler_params=pltpu.CompilerParams(vmem_limit_bytes=VMEM_LIMIT),
        cost_estimate=pl.CostEstimate(flops=a.size, bytes_accessed=12 * a.size, transcendentals=0),
        name="combine",
    )(here, a, b)


def place_kernel(space, here_ref, *refs):
    parts, out = refs[:-1], refs[-1]
    for k, part in enumerate(parts):
        group = here_ref[0] - k
        group = jnp.where(group < 0, group + space, group)
        out[group] = part[...]


def place(here, parts):
    space = len(parts)
    own, columns = parts[0].shape
    return pl.pallas_call(
        functools.partial(place_kernel, space),
        out_shape=jax.ShapeDtypeStruct((space, own, columns), jnp.float32),
        in_specs=[SMEM_SPEC] + [VMEM_SPEC] * space,
        out_specs=VMEM_SPEC,
        compiler_params=pltpu.CompilerParams(vmem_limit_bytes=VMEM_LIMIT),
        cost_estimate=pl.CostEstimate(flops=0, bytes_accessed=8 * space * own * columns, transcendentals=0),
        name="place",
    )(here, *parts)


def rotate(x, axis, step):
    size = lax.axis_size(axis)
    return lax.ppermute(x, axis, [(i, (i + step) % size) for i in range(size)])


def shards(orbitals, potential):
    space = lax.axis_size("space")
    band = lax.axis_size("band")
    count, layers, plane = orbitals.shape
    tiles = plane // LANES
    rows = tiles * layers
    share = rows // band
    own = count // space
    chunk = max(c for c in range(1, SUBLANES + 1) if own % c == 0)
    chunks = own // chunk

    s_index = lax.axis_index("space")
    b_index = lax.axis_index("band")
    here = jnp.stack([s_index, b_index])

    def as_rows(x):
        n = x.shape[0]
        return x.reshape(n, layers, tiles, LANES).transpose(0, 2, 1, 3).reshape(n * rows, LANES)

    matrix = jnp.asarray(plane_matrix())
    own_v = as_rows(potential[None])
    vs = [own_v] + [rotate(own_v, "space", space - k) for k in range(1, space)]
    arrived = as_rows(lax.all_to_all(orbitals, "space", split_axis=0, concat_axis=0, tiled=True))

    def filtered(c, x):
        outs = run_filter(here, x, matrix, vs, c * chunk, space, layers, tiles, chunk)
        return [outs[0]] + [rotate(outs[k], "space", k) for k in range(1, space)]

    made = [filtered(c, arrived) for c in range(min(chunks, 2))]
    made[0], made[-1][0] = lax.optimization_barrier((made[0], made[-1][0]))
    head = pack(here, made[0], space, band, share, chunk, 1, False)[0]
    head, arrived = lax.optimization_barrier((head, arrived))
    parts = [lax.all_to_all(head, "band", split_axis=0, concat_axis=0, tiled=True)]
    places = [(0, 1, False)]
    made += [filtered(c, arrived) for c in range(2, chunks)]
    if chunks > 1:
        late = [made[c][k] for k in range(space) for c in range(1, chunks)]
        packed = pack(here, late, space, band, share, chunk, chunks - 1, True)
        got = {0: packed[0]}
        for k in reversed(range(1, band)):
            got[k] = exchange(packed[k], "band", k)
        parts += [got[k] for k in range(band)]
        places.append((chunk, chunks - 1, True))
    blocks = [made[c][k] for k in range(space) for c in range(chunks)]

    result = unpack(here, blocks, space, rows, chunk, [chunks])
    parts[-1], result = lax.optimization_barrier((parts[-1], result))
    result = result.reshape(count, tiles, layers, LANES).transpose(0, 2, 1, 3).reshape(count, layers, plane)

    pairs = band // 2
    core = b_index % 2
    pair = b_index // 2

    own_half, other = gram(jnp.stack([core, b_index]), parts, band, count, space, chunk, places)
    other = lax.ppermute(other, "band", [(i, i ^ 1) for i in range(band)])
    split = (pairs, space, own, band * count)
    sums = combine(here, own_half.reshape(split), other.reshape(split))

    mine = sums[0]
    for k in range(1, space):
        mine = mine + rotate(sums[k], "space", k)

    final = lax.dynamic_index_in_dim(mine, pair, 0, keepdims=False)
    for k in range(1, pairs):
        sent = lax.dynamic_index_in_dim(mine, partner(pair, pairs, k), 0, keepdims=False)
        final = final + exchange(sent, "band", k, 2)
    final = final * (1.0 / (layers * space * plane))

    margin = place(here, [final] + [rotate(final, "space", k) for k in range(1, space)])
    return result, margin.reshape(count, band * count)


def solution(mesh):
    return jax.shard_map(
        shards,
        mesh=mesh,
        in_specs=(P("band", "space", None), P("space", None)),
        out_specs=(P("band", "space", None), P("band", None)),
        check_vma=False,
    )
```

```python
import functools

import jax
import jax.numpy as jnp
import ml_dtypes
import numpy as np
from jax import lax
from jax.experimental import pallas as pl
from jax.experimental.pallas import tpu as pltpu
from jax.sharding import PartitionSpec as P

NZ = 64
LANES = 128
SUBLANES = 8
VMEM_LIMIT = 12 * 1024 * 1024
PARTS = 2


def plane_matrix():
    wide = 2 * LANES
    matrix = np.zeros((2 * wide, wide), np.float32)
    for y in range(wide // NZ):
        for z in range(NZ):
            column = y * NZ + z
            for step, weight in ((1, -16.0), (-1, -16.0), (2, 1.0), (-2, 1.0)):
                matrix[y * NZ + (z + step) % NZ, column] += weight
                row = y + step
                if row < 0:
                    row += 6
                elif row >= 4:
                    row += 2
                matrix[row * NZ + z, column] += weight
    return matrix.astype(ml_dtypes.bfloat16)


def filter_kernel(space, layers, tiles, chunk, pitch, offset, x_ref, m_ref, *refs):
    f0, f1, coef, mm, hi, lo = refs[-6:]
    rows = tiles * layers
    if len(refs) == 2 * space + 7:
        joined = refs[2 * space]
        for s in range(space):
            joined[s * rows : (s + 1) * rows, :] = refs[s][...]
        out_refs = refs[space : 2 * space]
    else:
        joined, out_refs = refs[0], refs[1 : 1 + space]
    planes = space * layers
    quads, height, wide = f0.shape
    here = lax.axis_index("space")

    def put(f, j, v):
        f[j] = v
        top = v.astype(jnp.bfloat16)
        hi[j] = top
        lo[j] = (v - top.astype(jnp.float32)).astype(jnp.bfloat16)

    for j in range(quads):
        columns = []
        for half in range(2):
            column = []
            for p in range(planes):
                s, l = divmod(p, layers)
                row = (2 * j + half) * layers + l
                slab = here + s
                slab = jnp.where(slab >= space, slab - space, slab)
                column.append(x_ref[pl.ds((slab * pitch + offset) * rows + row, chunk, stride=rows), :])
                w = joined[s * rows + row : s * rows + row + 1, :]
                coef[j, p * chunk : (p + 1) * chunk, half * LANES : (half + 1) * LANES] = jnp.broadcast_to(
                    0.5 * w - 1.125, (chunk, LANES)
                )
            columns.append(jnp.concatenate(column, axis=0))
        put(f0, j, jnp.concatenate(columns, axis=1))

    def beside(a):
        before = jnp.concatenate([a[quads - 1 :], a[: quads - 1]], axis=0)
        after = jnp.concatenate([a[1:], a[:1]], axis=0)
        return jnp.concatenate([before[:, :, LANES:], after[:, :, :LANES]], axis=2)

    def product():
        top, rest = hi[...], lo[...]
        left = jnp.concatenate([top, beside(top), rest, beside(rest)], axis=2).reshape(quads * height, 4 * wide)
        right = jnp.concatenate([m_ref[...], m_ref[...]], axis=0)
        got = lax.dot_general(left, right, (((1,), (0,)), ((), ())), preferred_element_type=jnp.float32)
        mm[...] = got.reshape(quads, height, wide)

    def stencil(f, j):
        v = f[j]

        def moved(k):
            k = k % planes * chunk
            return jnp.concatenate([v[k:], v[:k]], axis=0) if k else v

        return v, (mm[j] + (moved(2) + moved(-2))) - 16.0 * (moved(1) + moved(-1))

    product()
    for j in range(quads):
        v, s = stencil(f0, j)
        put(f1, j, (1.0 / 96.0) * s + 0.5 * (coef[j] * v))
    product()
    for j in range(quads):
        v, s = stencil(f1, j)
        put(f0, j, ((1.0 / 48.0) * s + coef[j] * v) - f0[j])
    product()
    for j in range(quads):
        v, s = stencil(f0, j)
        y = ((1.0 / 48.0) * s + coef[j] * v) - f1[j]
        for p in range(planes):
            for half in range(2):
                block = y[p * chunk : (p + 1) * chunk, half * LANES : (half + 1) * LANES]
                out_refs[p // layers][(2 * j + half) * layers + p % layers] = block


VMEM_SPEC = pl.BlockSpec(memory_space=pltpu.VMEM)


def run_filter(x, matrix, vs, offset, space, layers, tiles, chunk):
    rows = tiles * layers
    planes = space * layers
    pitch = x.shape[0] // (space * rows)
    shape = (tiles // 2, planes * chunk, 2 * LANES)
    out_shape = [jax.ShapeDtypeStruct((rows, chunk, LANES), jnp.float32)] * space
    if len(vs) > 1:
        out_shape.append(jax.ShapeDtypeStruct((space * rows, LANES), jnp.float32))
    return pl.pallas_call(
        functools.partial(filter_kernel, space, layers, tiles, chunk, pitch, offset),
        out_shape=out_shape,
        in_specs=[VMEM_SPEC] * (2 + len(vs)),
        out_specs=[VMEM_SPEC] * len(out_shape),
        scratch_shapes=[pltpu.VMEM(shape, jnp.float32)] * 4 + [pltpu.VMEM(shape, jnp.bfloat16)] * 2,
        compiler_params=pltpu.CompilerParams(vmem_limit_bytes=VMEM_LIMIT),
        cost_estimate=pl.CostEstimate(
            flops=50 * planes * tiles * SUBLANES * LANES,
            bytes_accessed=2 * planes * tiles * chunk * LANES * 4,
            transcendentals=0,
        ),
        name="filter",
    )(x, matrix, *vs)


def partner(index, size, k, forward=True):
    if size & (size - 1) == 0:
        return index ^ k
    moved = index + k if forward else index - k + size
    return jnp.where(moved >= size, moved - size, moved)


def exchange(x, axis, k, pitch=1):
    size = lax.axis_size(axis) // pitch
    power = size & (size - 1) == 0
    pairs = []
    for i in range(size):
        target = i ^ k if power else (i + k) % size
        pairs += [(i * pitch + low, target * pitch + low) for low in range(pitch)]
    return lax.ppermute(x, axis, pairs)


def pack_kernel(space, band, share, chunk, subs, *refs):
    blocks, outs = refs[: space * subs], refs[space * subs :]
    here, mine = lax.axis_index("space"), lax.axis_index("band")
    for k in range(space):
        group = here - k
        group = jnp.where(group < 0, group + space, group)
        for sub in range(subs):
            first = pl.multiple_of((group * subs + sub) * chunk, chunk)
            block = blocks[k * subs + sub]
            for step in range(band):
                out = outs[0].at[step] if len(outs) == 1 else outs[step]
                target = step if len(outs) == 1 else partner(mine, band, step)
                for q in range(share):
                    out[pl.ds(first, chunk), q * LANES : (q + 1) * LANES] = block[target * share + q]


def pack(blocks, space, band, share, chunk, subs, apart):
    shape = (space * subs * chunk, share * LANES)
    out_shape = [jax.ShapeDtypeStruct(shape, jnp.float32)] * band
    if not apart:
        out_shape = [jax.ShapeDtypeStruct((band,) + shape, jnp.float32)]
    return pl.pallas_call(
        functools.partial(pack_kernel, space, band, share, chunk, subs),
        out_shape=out_shape,
        in_specs=[VMEM_SPEC] * len(blocks),
        out_specs=[VMEM_SPEC] * len(out_shape),
        compiler_params=pltpu.CompilerParams(vmem_limit_bytes=VMEM_LIMIT),
        cost_estimate=pl.CostEstimate(
            flops=0, bytes_accessed=8 * band * space * subs * chunk * share * LANES, transcendentals=0
        ),
        name="pack",
    )(*blocks)


def unpack_kernel(space, rows, chunk, subs_of, *refs):
    blocks, out = refs[:-1], refs[-1]
    here = lax.axis_index("space")
    start = 0
    taken = 0
    for subs in subs_of:
        for k in range(space):
            group = here - k
            group = jnp.where(group < 0, group + space, group)
            for sub in range(subs):
                block = blocks[taken + k * subs + sub]
                first = (start + (group * subs + sub) * chunk) * rows
                for row in range(rows):
                    out[pl.ds(first + row, chunk, stride=rows), :] = block[row]
        taken += space * subs
        start += space * subs * chunk


def unpack(blocks, space, rows, chunk, subs_of):
    count = sum(subs_of) * space * chunk
    return pl.pallas_call(
        functools.partial(unpack_kernel, space, rows, chunk, subs_of),
        out_shape=jax.ShapeDtypeStruct((count * rows, LANES), jnp.float32),
        in_specs=[VMEM_SPEC] * len(blocks),
        out_specs=VMEM_SPEC,
        compiler_params=pltpu.CompilerParams(vmem_limit_bytes=VMEM_LIMIT),
        cost_estimate=pl.CostEstimate(flops=0, bytes_accessed=8 * count * rows * LANES, transcendentals=0),
        name="unpack",
    )(*blocks)


def half_product(band, count, which, hi, lo, first, out):
    def picked(x):
        return jnp.concatenate([x[2 * z + which] for z in range(band // 2)], axis=0)

    def dot(a, b):
        return lax.dot_general(a, b, (((1,), (1,)), ((), ())), preferred_element_type=jnp.float32)

    cells = hi.shape[-1]
    left_hi, left_lo = picked(hi), picked(lo)
    width = out.shape[1]
    bands = slice(first // count, (first + width) // count)
    right_hi = hi[bands].reshape(width, cells)
    right_lo = lo[bands].reshape(width, cells)
    for c in range(0, width, 256):
        columns = slice(c, min(c + 256, width))
        top, rest = right_hi[columns], right_lo[columns]
        out[:, columns] = dot(left_hi, top) + (dot(left_hi, rest) + dot(left_lo, top))


def gram_kernel(band, count, space, chunk, places, *refs):
    parts, (*outs, hi, lo, wide) = list(refs[: -3 - PARTS]), refs[-3 - PARTS :]
    own = count // space
    mine = lax.axis_index("band")
    for offset, subs, apart in places:
        size = subs * chunk
        taken = [parts.pop(0) for _ in range(band)] if apart else parts.pop(0)
        for step in range(band):
            source = partner(mine, band, step, forward=False) if apart else step
            for g in range(space):
                wide[source, g * own + offset : g * own + offset + size, :] = taken[step][g * size : (g + 1) * size, :]
    for b in range(band):
        top = wide[b].astype(jnp.bfloat16)
        hi[b] = top
        lo[b] = (wide[b] - top.astype(jnp.float32)).astype(jnp.bfloat16)
    for n, out in enumerate(outs):
        half_product(band, count, 1 - mine % 2, hi, lo, n * out.shape[1], out)


def own_gram_kernel(band, count, first, hi, lo, out):
    half_product(band, count, lax.axis_index("band") % 2, hi, lo, first, out)


def gram(parts, band, count, space, chunk, places):
    cells = parts[0].shape[-1]
    half = jax.ShapeDtypeStruct((band // 2 * count, band * count // PARTS), jnp.float32)
    narrow = jax.ShapeDtypeStruct((band, count, cells), jnp.bfloat16)
    return pl.pallas_call(
        functools.partial(gram_kernel, band, count, space, chunk, places),
        out_shape=[half] * PARTS + [narrow, narrow],
        in_specs=[VMEM_SPEC] * len(parts),
        out_specs=[VMEM_SPEC] * (PARTS + 2),
        scratch_shapes=[pltpu.VMEM((band, count, cells), jnp.float32)],
        compiler_params=pltpu.CompilerParams(vmem_limit_bytes=VMEM_LIMIT),
        cost_estimate=pl.CostEstimate(
            flops=3 * band * band * count * count * cells,
            bytes_accessed=4 * band * count * (cells + band * count // 2),
            transcendentals=0,
        ),
        name="gram",
    )(*parts)


def own_gram(hi, lo, first, width):
    band, count, cells = hi.shape
    return pl.pallas_call(
        functools.partial(own_gram_kernel, band, count, first),
        out_shape=jax.ShapeDtypeStruct((band // 2 * count, width), jnp.float32),
        in_specs=[VMEM_SPEC] * 2,
        out_specs=VMEM_SPEC,
        compiler_params=pltpu.CompilerParams(vmem_limit_bytes=VMEM_LIMIT),
        cost_estimate=pl.CostEstimate(
            flops=3 * band * count * width * cells, bytes_accessed=4 * band * count * cells, transcendentals=0
        ),
        name="own_gram",
    )(hi, lo)


def combine_kernel(space, a_ref, b_ref, *outs):
    for k, out in enumerate(outs):
        group = lax.axis_index("space") + k
        group = jnp.where(group >= space, group - space, group)
        for z in range(out.shape[0]):
            out[z] = a_ref[z, group] + b_ref[z, group]


def combine(a, b):
    pairs, space, own, columns = a.shape
    return pl.pallas_call(
        functools.partial(combine_kernel, space),
        out_shape=[jax.ShapeDtypeStruct((pairs, own, columns), jnp.float32)] * space,
        in_specs=[VMEM_SPEC] * 2,
        out_specs=[VMEM_SPEC] * space,
        compiler_params=pltpu.CompilerParams(vmem_limit_bytes=VMEM_LIMIT),
        cost_estimate=pl.CostEstimate(flops=a.size, bytes_accessed=12 * a.size, transcendentals=0),
        name="combine",
    )(a, b)


def place_kernel(space, *refs):
    parts, out = refs[:-1], refs[-1]
    width = parts[0].shape[1]
    for n, part in enumerate(parts):
        h, k = divmod(n, space)
        group = lax.axis_index("space") - k
        group = jnp.where(group < 0, group + space, group)
        out[group, :, h * width : (h + 1) * width] = part[...]


def place(parts, space):
    own, width = parts[0].shape
    columns = width * len(parts) // space
    return pl.pallas_call(
        functools.partial(place_kernel, space),
        out_shape=jax.ShapeDtypeStruct((space, own, columns), jnp.float32),
        in_specs=[VMEM_SPEC] * len(parts),
        out_specs=VMEM_SPEC,
        compiler_params=pltpu.CompilerParams(vmem_limit_bytes=VMEM_LIMIT),
        cost_estimate=pl.CostEstimate(flops=0, bytes_accessed=8 * space * own * columns, transcendentals=0),
        name="place",
    )(*parts)


def rotate(x, axis, step):
    size = lax.axis_size(axis)
    return lax.ppermute(x, axis, [(i, (i + step) % size) for i in range(size)])


def shards(orbitals, potential):
    space = lax.axis_size("space")
    band = lax.axis_size("band")
    count, layers, plane = orbitals.shape
    tiles = plane // LANES
    rows = tiles * layers
    share = rows // band
    own = count // space
    chunk = max(c for c in range(1, SUBLANES + 1) if own % c == 0)
    chunks = own // chunk


    def as_rows(x):
        n = x.shape[0]
        return x.reshape(n, layers, tiles, LANES).transpose(0, 2, 1, 3).reshape(n * rows, LANES)

    matrix = jnp.asarray(plane_matrix())
    own_v = as_rows(potential[None])
    vs = [own_v] + [rotate(own_v, "space", space - k) for k in range(1, space)]
    arrived = as_rows(lax.all_to_all(orbitals, "space", split_axis=0, concat_axis=0, tiled=True))

    def filtered(c, x):
        outs = run_filter(x, matrix, vs, c * chunk, space, layers, tiles, chunk)
        vs[:] = [outs[-1]] if len(vs) > 1 else vs
        return [outs[0]] + [rotate(outs[k], "space", k) for k in range(1, space)]

    made = [filtered(c, arrived) for c in range(min(chunks, 2))]
    made[0], made[-1][0] = lax.optimization_barrier((made[0], made[-1][0]))
    head = pack(made[0], space, band, share, chunk, 1, False)[0]
    head, arrived = lax.optimization_barrier((head, arrived))
    parts = [lax.all_to_all(head, "band", split_axis=0, concat_axis=0, tiled=True)]
    places = [(0, 1, False)]
    made += [filtered(c, arrived) for c in range(2, chunks)]
    if chunks > 1:
        late = [made[c][k] for k in range(space) for c in range(1, chunks)]
        packed = pack(late, space, band, share, chunk, chunks - 1, True)
        got = {0: packed[0]}
        for k in reversed(range(1, band)):
            got[k] = exchange(packed[k], "band", k)
        parts += [got[k] for k in range(band)]
        places.append((chunk, chunks - 1, True))
    blocks = [made[c][k] for k in range(space) for c in range(chunks)]

    result = unpack(blocks, space, rows, chunk, [chunks])
    parts[-1], result = lax.optimization_barrier((parts[-1], result))
    result = result.reshape(count, tiles, layers, LANES).transpose(0, 2, 1, 3).reshape(count, layers, plane)

    pairs = band // 2
    pair = lax.axis_index("band") // 2
    scale = 1.0 / (layers * space * plane)

    *others, hi, lo = gram(parts, band, count, space, chunk, places)
    others = [lax.ppermute(x, "band", [(i, i ^ 1) for i in range(band)]) for x in others]
    width = band * count // PARTS
    split = (pairs, space, own, width)
    placed = []
    for h in range(PARTS):
        sums = combine(own_gram(hi, lo, h * width, width).reshape(split), others[h].reshape(split))
        sums, hi = lax.optimization_barrier((sums, hi))
        mine = sums[0]
        for k in range(1, space):
            mine = mine + rotate(sums[k], "space", k)
        final = lax.dynamic_index_in_dim(mine, pair, 0, keepdims=False)
        for k in range(1, pairs):
            sent = lax.dynamic_index_in_dim(mine, partner(pair, pairs, k), 0, keepdims=False)
            final = final + exchange(sent, "band", k, 2)
        final = final * scale
        placed += [final] + [rotate(final, "space", k) for k in range(1, space)]
    return result, place(placed, space).reshape(count, band * count)


def solution(mesh):
    return jax.shard_map(
        shards,
        mesh=mesh,
        in_specs=(P("band", "space", None), P("space", None)),
        out_specs=(P("band", "space", None), P("band", None)),
        check_vma=False,
    )
```

```python
import functools

import jax
import jax.numpy as jnp
import ml_dtypes
import numpy as np
from jax import lax
from jax.experimental import pallas as pl
from jax.experimental.pallas import tpu as pltpu
from jax.sharding import PartitionSpec as P

NZ = 64
LANES = 128
SUBLANES = 8
VMEM_LIMIT = 12 * 1024 * 1024
PARTS = 2


def plane_matrix():
    wide = 2 * LANES
    matrix = np.zeros((2 * wide, wide), np.float32)
    for y in range(wide // NZ):
        for z in range(NZ):
            column = y * NZ + z
            for step, weight in ((1, -16.0), (-1, -16.0), (2, 1.0), (-2, 1.0)):
                matrix[y * NZ + (z + step) % NZ, column] += weight
                row = y + step
                if row < 0:
                    row += 6
                elif row >= 4:
                    row += 2
                matrix[row * NZ + z, column] += weight
    return matrix.astype(ml_dtypes.bfloat16)


def filter_kernel(space, layers, tiles, chunk, pitch, offset, x_ref, m_ref, *refs):
    f0, f1, coef, mm, hi, lo = refs[-6:]
    rows = tiles * layers
    if len(refs) == 2 * space + 7:
        joined = refs[2 * space]
        for s in range(space):
            joined[s * rows : (s + 1) * rows, :] = refs[s][...]
        out_refs = refs[space : 2 * space]
    else:
        joined, out_refs = refs[0], refs[1 : 1 + space]
    planes = space * layers
    quads, height, wide = f0.shape
    here = lax.axis_index("space")

    def put(f, j, v):
        f[j] = v
        top = v.astype(jnp.bfloat16)
        hi[j] = top
        lo[j] = (v - top.astype(jnp.float32)).astype(jnp.bfloat16)

    for j in range(quads):
        columns = []
        for half in range(2):
            column = []
            for p in range(planes):
                s, l = divmod(p, layers)
                row = (2 * j + half) * layers + l
                slab = here + s
                slab = jnp.where(slab >= space, slab - space, slab)
                column.append(x_ref[pl.ds((slab * pitch + offset) * rows + row, chunk, stride=rows), :])
                w = joined[s * rows + row : s * rows + row + 1, :]
                coef[j, p * chunk : (p + 1) * chunk, half * LANES : (half + 1) * LANES] = jnp.broadcast_to(
                    0.5 * w - 1.125, (chunk, LANES)
                )
            columns.append(jnp.concatenate(column, axis=0))
        put(f0, j, jnp.concatenate(columns, axis=1))

    def beside(a):
        before = jnp.concatenate([a[quads - 1 :], a[: quads - 1]], axis=0)
        after = jnp.concatenate([a[1:], a[:1]], axis=0)
        return jnp.concatenate([before[:, :, LANES:], after[:, :, :LANES]], axis=2)

    def product():
        top, rest = hi[...], lo[...]
        left = jnp.concatenate([top, beside(top), rest, beside(rest)], axis=2).reshape(quads * height, 4 * wide)
        right = jnp.concatenate([m_ref[...], m_ref[...]], axis=0)
        got = lax.dot_general(left, right, (((1,), (0,)), ((), ())), preferred_element_type=jnp.float32)
        mm[...] = got.reshape(quads, height, wide)

    def stencil(f, j):
        v = f[j]

        def moved(k):
            k = k % planes * chunk
            return jnp.concatenate([v[k:], v[:k]], axis=0) if k else v

        return v, (mm[j] + (moved(2) + moved(-2))) - 16.0 * (moved(1) + moved(-1))

    product()
    for j in range(quads):
        v, s = stencil(f0, j)
        put(f1, j, (1.0 / 96.0) * s + 0.5 * (coef[j] * v))
    product()
    for j in range(quads):
        v, s = stencil(f1, j)
        put(f0, j, ((1.0 / 48.0) * s + coef[j] * v) - f0[j])
    product()
    for j in range(quads):
        v, s = stencil(f0, j)
        y = ((1.0 / 48.0) * s + coef[j] * v) - f1[j]
        for p in range(planes):
            for half in range(2):
                block = y[p * chunk : (p + 1) * chunk, half * LANES : (half + 1) * LANES]
                out_refs[p // layers][(2 * j + half) * layers + p % layers] = block


VMEM_SPEC = pl.BlockSpec(memory_space=pltpu.VMEM)


def run_filter(x, matrix, vs, offset, space, layers, tiles, chunk):
    rows = tiles * layers
    planes = space * layers
    pitch = x.shape[0] // (space * rows)
    shape = (tiles // 2, planes * chunk, 2 * LANES)
    out_shape = [jax.ShapeDtypeStruct((rows, chunk, LANES), jnp.float32)] * space
    if len(vs) > 1:
        out_shape.append(jax.ShapeDtypeStruct((space * rows, LANES), jnp.float32))
    return pl.pallas_call(
        functools.partial(filter_kernel, space, layers, tiles, chunk, pitch, offset),
        out_shape=out_shape,
        in_specs=[VMEM_SPEC] * (2 + len(vs)),
        out_specs=[VMEM_SPEC] * len(out_shape),
        scratch_shapes=[pltpu.VMEM(shape, jnp.float32)] * 4 + [pltpu.VMEM(shape, jnp.bfloat16)] * 2,
        compiler_params=pltpu.CompilerParams(vmem_limit_bytes=VMEM_LIMIT),
        cost_estimate=pl.CostEstimate(
            flops=50 * planes * tiles * SUBLANES * LANES,
            bytes_accessed=2 * planes * tiles * chunk * LANES * 4,
            transcendentals=0,
        ),
        name="filter",
    )(x, matrix, *vs)


def partner(index, size, k, forward=True):
    if size & (size - 1) == 0:
        return index ^ k
    moved = index + k if forward else index - k + size
    return jnp.where(moved >= size, moved - size, moved)


def exchange(x, axis, k, pitch=1):
    size = lax.axis_size(axis) // pitch
    power = size & (size - 1) == 0
    pairs = []
    for i in range(size):
        target = i ^ k if power else (i + k) % size
        pairs += [(i * pitch + low, target * pitch + low) for low in range(pitch)]
    return lax.ppermute(x, axis, pairs)


def pack_kernel(space, band, share, chunk, subs, *refs):
    blocks, outs = refs[: space * subs], refs[space * subs :]
    here, mine = lax.axis_index("space"), lax.axis_index("band")
    for k in range(space):
        group = here - k
        group = jnp.where(group < 0, group + space, group)
        for sub in range(subs):
            first = pl.multiple_of((group * subs + sub) * chunk, chunk)
            block = blocks[k * subs + sub]
            for step in range(band):
                out = outs[0].at[step] if len(outs) == 1 else outs[step]
                target = step if len(outs) == 1 else partner(mine, band, step)
                for q in range(share):
                    out[pl.ds(first, chunk), q * LANES : (q + 1) * LANES] = block[target * share + q]


def pack(blocks, space, band, share, chunk, subs, apart):
    shape = (space * subs * chunk, share * LANES)
    out_shape = [jax.ShapeDtypeStruct(shape, jnp.float32)] * band
    if not apart:
        out_shape = [jax.ShapeDtypeStruct((band,) + shape, jnp.float32)]
    return pl.pallas_call(
        functools.partial(pack_kernel, space, band, share, chunk, subs),
        out_shape=out_shape,
        in_specs=[VMEM_SPEC] * len(blocks),
        out_specs=[VMEM_SPEC] * len(out_shape),
        compiler_params=pltpu.CompilerParams(vmem_limit_bytes=VMEM_LIMIT),
        cost_estimate=pl.CostEstimate(
            flops=0, bytes_accessed=8 * band * space * subs * chunk * share * LANES, transcendentals=0
        ),
        name="pack",
    )(*blocks)


def unpack_kernel(space, rows, chunk, subs_of, *refs):
    blocks, out = refs[:-1], refs[-1]
    here = lax.axis_index("space")
    start = 0
    taken = 0
    for subs in subs_of:
        for k in range(space):
            group = here - k
            group = jnp.where(group < 0, group + space, group)
            for sub in range(subs):
                block = blocks[taken + k * subs + sub]
                first = (start + (group * subs + sub) * chunk) * rows
                for row in range(rows):
                    out[pl.ds(first + row, chunk, stride=rows), :] = block[row]
        taken += space * subs
        start += space * subs * chunk


def unpack(blocks, space, rows, chunk, subs_of):
    count = sum(subs_of) * space * chunk
    return pl.pallas_call(
        functools.partial(unpack_kernel, space, rows, chunk, subs_of),
        out_shape=jax.ShapeDtypeStruct((count * rows, LANES), jnp.float32),
        in_specs=[VMEM_SPEC] * len(blocks),
        out_specs=VMEM_SPEC,
        compiler_params=pltpu.CompilerParams(vmem_limit_bytes=VMEM_LIMIT),
        cost_estimate=pl.CostEstimate(flops=0, bytes_accessed=8 * count * rows * LANES, transcendentals=0),
        name="unpack",
    )(*blocks)


def half_product(band, count, which, hi, lo, first, out):
    def picked(x):
        return jnp.concatenate([x[2 * z + which] for z in range(band // 2)], axis=0)

    def dot(a, b):
        return lax.dot_general(a, b, (((1,), (1,)), ((), ())), preferred_element_type=jnp.float32)

    cells = hi.shape[-1]
    left_hi, left_lo = picked(hi), picked(lo)
    width = out.shape[1]
    bands = slice(first // count, (first + width) // count)
    right_hi = hi[bands].reshape(width, cells)
    right_lo = lo[bands].reshape(width, cells)
    for c in range(0, width, 256):
        columns = slice(c, min(c + 256, width))
        top, rest = right_hi[columns], right_lo[columns]
        out[:, columns] = dot(left_hi, top) + (dot(left_hi, rest) + dot(left_lo, top))


def gram_kernel(band, count, space, chunk, places, *refs):
    parts, (*outs, hi, lo, wide, done) = list(refs[: -4 - PARTS]), refs[-4 - PARTS :]
    own = count // space
    mine = lax.axis_index("band")
    copies = []
    for offset, subs, apart in reversed(places):
        size = subs * chunk
        taken = [parts.pop() for _ in range(band)][::-1] if apart else parts.pop()
        for step in range(band):
            source = partner(mine, band, step, forward=False) if apart else step
            for g in range(space):
                rows = slice(g * own + offset, g * own + offset + size)
                if apart:
                    from_ref = taken[step].at[g * size : (g + 1) * size, :]
                    copies.append(pltpu.make_async_copy(from_ref, wide.at[source, rows, :], done.at[len(copies)]))
                    copies[-1].start()
                else:
                    wide[step, rows, :] = taken[step, g * size : (g + 1) * size, :]
    for copy in copies:
        copy.wait()
    for b in range(band):
        top = wide[b].astype(jnp.bfloat16)
        hi[b] = top
        lo[b] = (wide[b] - top.astype(jnp.float32)).astype(jnp.bfloat16)
    for n, out in enumerate(outs):
        half_product(band, count, 1 - mine % 2, hi, lo, n * out.shape[1], out)


def own_gram_kernel(band, count, first, hi, lo, out):
    half_product(band, count, lax.axis_index("band") % 2, hi, lo, first, out)


def gram(parts, band, count, space, chunk, places):
    cells = parts[0].shape[-1]
    half = jax.ShapeDtypeStruct((band // 2 * count, band * count // PARTS), jnp.float32)
    narrow = jax.ShapeDtypeStruct((band, count, cells), jnp.bfloat16)
    return pl.pallas_call(
        functools.partial(gram_kernel, band, count, space, chunk, places),
        out_shape=[half] * PARTS + [narrow, narrow],
        in_specs=[VMEM_SPEC] + [pl.BlockSpec(memory_space=pl.ANY)] * (len(parts) - 1),
        out_specs=[VMEM_SPEC] * (PARTS + 2),
        scratch_shapes=[
            pltpu.VMEM((band, count, cells), jnp.float32),
            pltpu.SemaphoreType.DMA((max(1, (len(parts) - 1) * space),)),
        ],
        compiler_params=pltpu.CompilerParams(vmem_limit_bytes=VMEM_LIMIT),
        cost_estimate=pl.CostEstimate(
            flops=3 * band * band * count * count * cells,
            bytes_accessed=4 * band * count * (cells + band * count // 2),
            transcendentals=0,
        ),
        name="gram",
    )(*parts)


def own_gram(hi, lo, first, width):
    band, count, cells = hi.shape
    return pl.pallas_call(
        functools.partial(own_gram_kernel, band, count, first),
        out_shape=jax.ShapeDtypeStruct((band // 2 * count, width), jnp.float32),
        in_specs=[VMEM_SPEC] * 2,
        out_specs=VMEM_SPEC,
        compiler_params=pltpu.CompilerParams(vmem_limit_bytes=VMEM_LIMIT),
        cost_estimate=pl.CostEstimate(
            flops=3 * band * count * width * cells, bytes_accessed=4 * band * count * cells, transcendentals=0
        ),
        name="own_gram",
    )(hi, lo)


def combine_kernel(space, a_ref, b_ref, *outs):
    for k, out in enumerate(outs):
        group = lax.axis_index("space") + k
        group = jnp.where(group >= space, group - space, group)
        for z in range(out.shape[0]):
            out[z] = a_ref[z, group] + b_ref[z, group]


def combine(a, b):
    pairs, space, own, columns = a.shape
    return pl.pallas_call(
        functools.partial(combine_kernel, space),
        out_shape=[jax.ShapeDtypeStruct((pairs, own, columns), jnp.float32)] * space,
        in_specs=[VMEM_SPEC] * 2,
        out_specs=[VMEM_SPEC] * space,
        compiler_params=pltpu.CompilerParams(vmem_limit_bytes=VMEM_LIMIT),
        cost_estimate=pl.CostEstimate(flops=a.size, bytes_accessed=12 * a.size, transcendentals=0),
        name="combine",
    )(a, b)


def place_kernel(space, *refs):
    parts, out = refs[:-1], refs[-1]
    width = parts[0].shape[1]
    for n, part in enumerate(parts):
        h, k = divmod(n, space)
        group = lax.axis_index("space") - k
        group = jnp.where(group < 0, group + space, group)
        out[group, :, h * width : (h + 1) * width] = part[...]


def place(parts, space):
    own, width = parts[0].shape
    columns = width * len(parts) // space
    return pl.pallas_call(
        functools.partial(place_kernel, space),
        out_shape=jax.ShapeDtypeStruct((space, own, columns), jnp.float32),
        in_specs=[VMEM_SPEC] * len(parts),
        out_specs=VMEM_SPEC,
        compiler_params=pltpu.CompilerParams(vmem_limit_bytes=VMEM_LIMIT),
        cost_estimate=pl.CostEstimate(flops=0, bytes_accessed=8 * space * own * columns, transcendentals=0),
        name="place",
    )(*parts)


def rotate(x, axis, step):
    size = lax.axis_size(axis)
    return lax.ppermute(x, axis, [(i, (i + step) % size) for i in range(size)])


def shards(orbitals, potential):
    space = lax.axis_size("space")
    band = lax.axis_size("band")
    count, layers, plane = orbitals.shape
    tiles = plane // LANES
    rows = tiles * layers
    share = rows // band
    own = count // space
    chunk = max(c for c in range(1, SUBLANES + 1) if own % c == 0)
    chunks = own // chunk


    def as_rows(x):
        n = x.shape[0]
        return x.reshape(n, layers, tiles, LANES).transpose(0, 2, 1, 3).reshape(n * rows, LANES)

    matrix = jnp.asarray(plane_matrix())
    own_v = as_rows(potential[None])
    vs = [own_v] + [rotate(own_v, "space", space - k) for k in range(1, space)]
    arrived = as_rows(lax.all_to_all(orbitals, "space", split_axis=0, concat_axis=0, tiled=True))

    def filtered(c, x):
        outs = run_filter(x, matrix, vs, c * chunk, space, layers, tiles, chunk)
        vs[:] = [outs[-1]] if len(vs) > 1 else vs
        return [outs[0]] + [rotate(outs[k], "space", k) for k in range(1, space)]

    made = [filtered(c, arrived) for c in range(chunks)]
    if chunks > 1:
        made[0], firsts = lax.optimization_barrier((made[0], [m[0] for m in made[1:]]))
        for m, first in zip(made[1:], firsts):
            m[0] = first
    head = pack(made[0], space, band, share, chunk, 1, False)[0]
    parts = [lax.all_to_all(head, "band", split_axis=0, concat_axis=0, tiled=True)]
    places = [(0, 1, False)]
    if chunks > 1:
        late = [made[c][k] for k in range(space) for c in range(1, chunks)]
        packed = pack(late, space, band, share, chunk, chunks - 1, True)
        got = {0: packed[0]}
        for k in reversed(range(1, band)):
            got[k] = exchange(packed[k], "band", k)
        parts += [got[k] for k in range(band)]
        places.append((chunk, chunks - 1, True))
    blocks = [made[c][k] for k in range(space) for c in range(chunks)]

    result = unpack(blocks, space, rows, chunk, [chunks])
    parts[-1], result = lax.optimization_barrier((parts[-1], result))
    result = result.reshape(count, tiles, layers, LANES).transpose(0, 2, 1, 3).reshape(count, layers, plane)

    pairs = band // 2
    pair = lax.axis_index("band") // 2
    scale = 1.0 / (layers * space * plane)

    *others, hi, lo = gram(parts, band, count, space, chunk, places)
    others = [lax.ppermute(x, "band", [(i, i ^ 1) for i in range(band)]) for x in others]
    width = band * count // PARTS
    split = (pairs, space, own, width)
    placed = []
    for h in range(PARTS):
        sums = combine(own_gram(hi, lo, h * width, width).reshape(split), others[h].reshape(split))
        sums, hi = lax.optimization_barrier((sums, hi))
        mine = sums[0]
        for k in range(1, space):
            mine = mine + rotate(sums[k], "space", k)
        final = lax.dynamic_index_in_dim(mine, pair, 0, keepdims=False)
        for k in range(1, pairs):
            sent = lax.dynamic_index_in_dim(mine, partner(pair, pairs, k), 0, keepdims=False)
            final = final + exchange(sent, "band", k, 2)
        final = final * scale
        placed += [final] + [rotate(final, "space", k) for k in range(1, space)]
    return result, place(placed, space).reshape(count, band * count)


def solution(mesh):
    return jax.shard_map(
        shards,
        mesh=mesh,
        in_specs=(P("band", "space", None), P("space", None)),
        out_specs=(P("band", "space", None), P("band", None)),
        check_vma=False,
    )
```

```python
import functools

import jax
import jax.numpy as jnp
import ml_dtypes
import numpy as np
from jax import lax
from jax.experimental import pallas as pl
from jax.experimental.pallas import tpu as pltpu
from jax.sharding import PartitionSpec as P

NZ = 64
LANES = 128
SUBLANES = 8
VMEM_LIMIT = 12 * 1024 * 1024
PARTS = 2


def plane_matrix():
    wide = 2 * LANES
    matrix = np.zeros((2 * wide, wide), np.float32)
    for y in range(wide // NZ):
        for z in range(NZ):
            column = y * NZ + z
            for step, weight in ((1, -16.0), (-1, -16.0), (2, 1.0), (-2, 1.0)):
                matrix[y * NZ + (z + step) % NZ, column] += weight
                row = y + step
                if row < 0:
                    row += 6
                elif row >= 4:
                    row += 2
                matrix[row * NZ + z, column] += weight
    return matrix.astype(ml_dtypes.bfloat16)


def filter_kernel(space, layers, tiles, chunk, pitch, offset, x_ref, m_ref, *refs):
    f0, f1, coef, mm, hi, lo = refs[-6:]
    rows = tiles * layers
    if len(refs) == 2 * space + 7:
        joined = refs[2 * space]
        for s in range(space):
            joined[s * rows : (s + 1) * rows, :] = refs[s][...]
        out_refs = refs[space : 2 * space]
    else:
        joined, out_refs = refs[0], refs[1 : 1 + space]
    planes = space * layers
    quads, height, wide = f0.shape
    here = lax.axis_index("space")

    def put(f, j, v):
        f[j] = v
        top = v.astype(jnp.bfloat16)
        hi[j] = top
        lo[j] = (v - top.astype(jnp.float32)).astype(jnp.bfloat16)

    for j in range(quads):
        columns = []
        for half in range(2):
            column = []
            for p in range(planes):
                s, l = divmod(p, layers)
                row = (2 * j + half) * layers + l
                slab = here + s
                slab = jnp.where(slab >= space, slab - space, slab)
                column.append(x_ref[pl.ds((slab * pitch + offset) * rows + row, chunk, stride=rows), :])
                w = joined[s * rows + row : s * rows + row + 1, :]
                coef[j, p * chunk : (p + 1) * chunk, half * LANES : (half + 1) * LANES] = jnp.broadcast_to(
                    0.5 * w - 1.125, (chunk, LANES)
                )
            columns.append(jnp.concatenate(column, axis=0))
        put(f0, j, jnp.concatenate(columns, axis=1))

    def beside(a):
        before = jnp.concatenate([a[quads - 1 :], a[: quads - 1]], axis=0)
        after = jnp.concatenate([a[1:], a[:1]], axis=0)
        return jnp.concatenate([before[:, :, LANES:], after[:, :, :LANES]], axis=2)

    def product():
        top, rest = hi[...], lo[...]
        left = jnp.concatenate([top, beside(top), rest, beside(rest)], axis=2).reshape(quads * height, 4 * wide)
        right = jnp.concatenate([m_ref[...], m_ref[...]], axis=0)
        got = lax.dot_general(left, right, (((1,), (0,)), ((), ())), preferred_element_type=jnp.float32)
        mm[...] = got.reshape(quads, height, wide)

    def stencil(f, j):
        v = f[j]

        def moved(k):
            k = k % planes * chunk
            return jnp.concatenate([v[k:], v[:k]], axis=0) if k else v

        return v, (mm[j] + (moved(2) + moved(-2))) - 16.0 * (moved(1) + moved(-1))

    product()
    for j in range(quads):
        v, s = stencil(f0, j)
        put(f1, j, (1.0 / 96.0) * s + 0.5 * (coef[j] * v))
    product()
    for j in range(quads):
        v, s = stencil(f1, j)
        put(f0, j, ((1.0 / 48.0) * s + coef[j] * v) - f0[j])
    product()
    for j in range(quads):
        v, s = stencil(f0, j)
        y = ((1.0 / 48.0) * s + coef[j] * v) - f1[j]
        for p in range(planes):
            for half in range(2):
                block = y[p * chunk : (p + 1) * chunk, half * LANES : (half + 1) * LANES]
                out_refs[p // layers][(2 * j + half) * layers + p % layers] = block


VMEM_SPEC = pl.BlockSpec(memory_space=pltpu.VMEM)


def run_filter(x, matrix, vs, offset, space, layers, tiles, chunk):
    rows = tiles * layers
    planes = space * layers
    pitch = x.shape[0] // (space * rows)
    shape = (tiles // 2, planes * chunk, 2 * LANES)
    out_shape = [jax.ShapeDtypeStruct((rows, chunk, LANES), jnp.float32)] * space
    if len(vs) > 1:
        out_shape.append(jax.ShapeDtypeStruct((space * rows, LANES), jnp.float32))
    return pl.pallas_call(
        functools.partial(filter_kernel, space, layers, tiles, chunk, pitch, offset),
        out_shape=out_shape,
        in_specs=[VMEM_SPEC] * (2 + len(vs)),
        out_specs=[VMEM_SPEC] * len(out_shape),
        scratch_shapes=[pltpu.VMEM(shape, jnp.float32)] * 4 + [pltpu.VMEM(shape, jnp.bfloat16)] * 2,
        compiler_params=pltpu.CompilerParams(vmem_limit_bytes=VMEM_LIMIT),
        cost_estimate=pl.CostEstimate(
            flops=50 * planes * tiles * SUBLANES * LANES,
            bytes_accessed=2 * planes * tiles * chunk * LANES * 4,
            transcendentals=0,
        ),
        name="filter",
    )(x, matrix, *vs)


def partner(index, size, k, forward=True):
    if size & (size - 1) == 0:
        return index ^ k
    moved = index + k if forward else index - k + size
    return jnp.where(moved >= size, moved - size, moved)


def exchange(x, axis, k, pitch=1):
    size = lax.axis_size(axis) // pitch
    power = size & (size - 1) == 0
    pairs = []
    for i in range(size):
        target = i ^ k if power else (i + k) % size
        pairs += [(i * pitch + low, target * pitch + low) for low in range(pitch)]
    return lax.ppermute(x, axis, pairs)


def pack_kernel(space, band, share, size, *refs):
    blocks, outs = refs[:space], refs[space:]
    here, mine = lax.axis_index("space"), lax.axis_index("band")
    for k, block in enumerate(blocks):
        group = here - k
        group = jnp.where(group < 0, group + space, group)
        first = pl.multiple_of(group * size, size)
        for step in range(band):
            out = outs[0].at[step] if len(outs) == 1 else outs[step]
            target = step if len(outs) == 1 else partner(mine, band, step)
            for q in range(share):
                out[pl.ds(first, size), q * LANES : (q + 1) * LANES] = block[target * share + q]


def pack(blocks, space, band, share, size, apart):
    shape = (space * size, share * LANES)
    out_shape = [jax.ShapeDtypeStruct(shape, jnp.float32)] * band
    if not apart:
        out_shape = [jax.ShapeDtypeStruct((band,) + shape, jnp.float32)]
    return pl.pallas_call(
        functools.partial(pack_kernel, space, band, share, size),
        out_shape=out_shape,
        in_specs=[VMEM_SPEC] * space,
        out_specs=[VMEM_SPEC] * len(out_shape),
        compiler_params=pltpu.CompilerParams(vmem_limit_bytes=VMEM_LIMIT),
        cost_estimate=pl.CostEstimate(
            flops=0, bytes_accessed=8 * band * space * size * share * LANES, transcendentals=0
        ),
        name="pack",
    )(*blocks)


def unpack_kernel(space, rows, own, sizes, *refs):
    blocks, out = refs[:-1], refs[-1]
    here = lax.axis_index("space")
    for n, block in enumerate(blocks):
        c, k = divmod(n, space)
        group = here - k
        group = jnp.where(group < 0, group + space, group)
        first = (group * own + sum(sizes[:c])) * rows
        for row in range(rows):
            out[pl.ds(first + row, sizes[c], stride=rows), :] = block[row]


def unpack(blocks, space, rows, sizes):
    own = sum(sizes)
    count = own * space
    return pl.pallas_call(
        functools.partial(unpack_kernel, space, rows, own, sizes),
        out_shape=jax.ShapeDtypeStruct((count * rows, LANES), jnp.float32),
        in_specs=[VMEM_SPEC] * len(blocks),
        out_specs=VMEM_SPEC,
        compiler_params=pltpu.CompilerParams(vmem_limit_bytes=VMEM_LIMIT),
        cost_estimate=pl.CostEstimate(flops=0, bytes_accessed=8 * count * rows * LANES, transcendentals=0),
        name="unpack",
    )(*blocks)


def half_product(band, count, which, hi, lo, first, out):
    def picked(x):
        return jnp.concatenate([x[2 * z + which] for z in range(band // 2)], axis=0)

    def dot(a, b):
        return lax.dot_general(a, b, (((1,), (1,)), ((), ())), preferred_element_type=jnp.float32)

    cells = hi.shape[-1]
    left_hi, left_lo = picked(hi), picked(lo)
    width = out.shape[1]
    bands = slice(first // count, (first + width) // count)
    right_hi = hi[bands].reshape(width, cells)
    right_lo = lo[bands].reshape(width, cells)
    for c in range(0, width, 256):
        columns = slice(c, min(c + 256, width))
        top, rest = right_hi[columns], right_lo[columns]
        out[:, columns] = dot(left_hi, top) + (dot(left_hi, rest) + dot(left_lo, top))


def gram_kernel(band, count, space, places, *refs):
    parts, (*outs, hi, lo, wide) = list(refs[: -3 - PARTS]), refs[-3 - PARTS :]
    own = count // space
    mine = lax.axis_index("band")
    for offset, size, apart in places:
        taken = [parts.pop(0) for _ in range(band)] if apart else parts.pop(0)
        for step in range(band):
            source = partner(mine, band, step, forward=False) if apart else step
            for g in range(space):
                wide[source, g * own + offset : g * own + offset + size, :] = taken[step][g * size : (g + 1) * size, :]
    for b in range(band):
        top = wide[b].astype(jnp.bfloat16)
        hi[b] = top
        lo[b] = (wide[b] - top.astype(jnp.float32)).astype(jnp.bfloat16)
    for n, out in enumerate(outs):
        half_product(band, count, 1 - mine % 2, hi, lo, n * out.shape[1], out)


def own_gram_kernel(band, count, first, hi, lo, out):
    half_product(band, count, lax.axis_index("band") % 2, hi, lo, first, out)


def gram(parts, band, count, space, places):
    cells = parts[0].shape[-1]
    half = jax.ShapeDtypeStruct((band // 2 * count, band * count // PARTS), jnp.float32)
    narrow = jax.ShapeDtypeStruct((band, count, cells), jnp.bfloat16)
    return pl.pallas_call(
        functools.partial(gram_kernel, band, count, space, places),
        out_shape=[half] * PARTS + [narrow, narrow],
        in_specs=[VMEM_SPEC] * len(parts),
        out_specs=[VMEM_SPEC] * (PARTS + 2),
        scratch_shapes=[pltpu.VMEM((band, count, cells), jnp.float32)],
        compiler_params=pltpu.CompilerParams(vmem_limit_bytes=VMEM_LIMIT),
        cost_estimate=pl.CostEstimate(
            flops=3 * band * band * count * count * cells,
            bytes_accessed=4 * band * count * (cells + band * count // 2),
            transcendentals=0,
        ),
        name="gram",
    )(*parts)


def own_gram(hi, lo, first, width):
    band, count, cells = hi.shape
    return pl.pallas_call(
        functools.partial(own_gram_kernel, band, count, first),
        out_shape=jax.ShapeDtypeStruct((band // 2 * count, width), jnp.float32),
        in_specs=[VMEM_SPEC] * 2,
        out_specs=VMEM_SPEC,
        compiler_params=pltpu.CompilerParams(vmem_limit_bytes=VMEM_LIMIT),
        cost_estimate=pl.CostEstimate(
            flops=3 * band * count * width * cells, bytes_accessed=4 * band * count * cells, transcendentals=0
        ),
        name="own_gram",
    )(hi, lo)


def combine_kernel(space, a_ref, b_ref, *outs):
    for k, out in enumerate(outs):
        group = lax.axis_index("space") + k
        group = jnp.where(group >= space, group - space, group)
        for z in range(out.shape[0]):
            out[z] = a_ref[z, group] + b_ref[z, group]


def combine(a, b):
    pairs, space, own, columns = a.shape
    return pl.pallas_call(
        functools.partial(combine_kernel, space),
        out_shape=[jax.ShapeDtypeStruct((pairs, own, columns), jnp.float32)] * space,
        in_specs=[VMEM_SPEC] * 2,
        out_specs=[VMEM_SPEC] * space,
        compiler_params=pltpu.CompilerParams(vmem_limit_bytes=VMEM_LIMIT),
        cost_estimate=pl.CostEstimate(flops=a.size, bytes_accessed=12 * a.size, transcendentals=0),
        name="combine",
    )(a, b)


def place_kernel(space, *refs):
    parts, out = refs[:-1], refs[-1]
    width = parts[0].shape[1]
    for n, part in enumerate(parts):
        h, k = divmod(n, space)
        group = lax.axis_index("space") - k
        group = jnp.where(group < 0, group + space, group)
        out[group, :, h * width : (h + 1) * width] = part[...]


def place(parts, space):
    own, width = parts[0].shape
    columns = width * len(parts) // space
    return pl.pallas_call(
        functools.partial(place_kernel, space),
        out_shape=jax.ShapeDtypeStruct((space, own, columns), jnp.float32),
        in_specs=[VMEM_SPEC] * len(parts),
        out_specs=VMEM_SPEC,
        compiler_params=pltpu.CompilerParams(vmem_limit_bytes=VMEM_LIMIT),
        cost_estimate=pl.CostEstimate(flops=0, bytes_accessed=8 * space * own * columns, transcendentals=0),
        name="place",
    )(*parts)


def rotate(x, axis, step):
    size = lax.axis_size(axis)
    return lax.ppermute(x, axis, [(i, (i + step) % size) for i in range(size)])


def shards(orbitals, potential):
    space = lax.axis_size("space")
    band = lax.axis_size("band")
    count, layers, plane = orbitals.shape
    tiles = plane // LANES
    rows = tiles * layers
    share = rows // band
    own = count // space
    chunk = max(c for c in range(1, SUBLANES + 1) if own % c == 0)
    sizes = [chunk] if own == chunk else [chunk, own - chunk]

    def as_rows(x):
        n = x.shape[0]
        return x.reshape(n, layers, tiles, LANES).transpose(0, 2, 1, 3).reshape(n * rows, LANES)

    matrix = jnp.asarray(plane_matrix())
    own_v = as_rows(potential[None])
    vs = [own_v] + [rotate(own_v, "space", space - k) for k in range(1, space)]
    arrived = as_rows(lax.all_to_all(orbitals, "space", split_axis=0, concat_axis=0, tiled=True))

    def filtered(offset, size):
        outs = run_filter(arrived, matrix, vs, offset, space, layers, tiles, size)
        vs[:] = [outs[-1]] if len(vs) > 1 else vs
        return [outs[0]] + [rotate(outs[k], "space", k) for k in range(1, space)]

    made = [filtered(sum(sizes[:c]), size) for c, size in enumerate(sizes)]
    if len(made) > 1:
        made[0], made[1][0] = lax.optimization_barrier((made[0], made[1][0]))
    head = pack(made[0], space, band, share, sizes[0], False)[0]
    head = lax.all_to_all(head, "band", split_axis=0, concat_axis=0, tiled=True)
    parts = [head]
    places = [(0, sizes[0], False)]
    if len(made) > 1:
        packed = pack(made[1], space, band, share, sizes[1], True)
        got = {0: packed[0]}
        for k in reversed(range(1, band)):
            got[k] = exchange(packed[k], "band", k)
        parts += [got[k] for k in range(band)]
        places.append((sizes[0], sizes[1], True))
        parts[0], made[0][0] = lax.optimization_barrier((parts[0], made[0][0]))

    result = unpack(sum(made, []), space, rows, sizes)
    parts[-1], result = lax.optimization_barrier((parts[-1], result))
    result = result.reshape(count, tiles, layers, LANES).transpose(0, 2, 1, 3).reshape(count, layers, plane)

    pairs = band // 2
    pair = lax.axis_index("band") // 2
    scale = 1.0 / (layers * space * plane)

    *others, hi, lo = gram(parts, band, count, space, places)
    others = [lax.ppermute(x, "band", [(i, i ^ 1) for i in range(band)]) for x in others]
    width = band * count // PARTS
    split = (pairs, space, own, width)
    placed = []
    for h in range(PARTS):
        sums = combine(own_gram(hi, lo, h * width, width).reshape(split), others[h].reshape(split))
        sums, hi = lax.optimization_barrier((sums, hi))
        mine = sums[0]
        for k in range(1, space):
            mine = mine + rotate(sums[k], "space", k)
        final = lax.dynamic_index_in_dim(mine, pair, 0, keepdims=False)
        for k in range(1, pairs):
            sent = lax.dynamic_index_in_dim(mine, partner(pair, pairs, k), 0, keepdims=False)
            final = final + exchange(sent, "band", k, 2)
        final = final * scale
        placed += [final] + [rotate(final, "space", k) for k in range(1, space)]
    return result, place(placed, space).reshape(count, band * count)


def solution(mesh):
    return jax.shard_map(
        shards,
        mesh=mesh,
        in_specs=(P("band", "space", None), P("space", None)),
        out_specs=(P("band", "space", None), P("band", None)),
        check_vma=False,
    )
```

```python
import functools

import jax
import jax.numpy as jnp
import ml_dtypes
import numpy as np
from jax import lax
from jax.experimental import pallas as pl
from jax.experimental.pallas import tpu as pltpu
from jax.sharding import PartitionSpec as P

NZ = 64
LANES = 128
SUBLANES = 8
VMEM_LIMIT = 12 * 1024 * 1024
PARTS = 2


def plane_matrix():
    wide = 2 * LANES
    matrix = np.zeros((2 * wide, wide), np.float32)
    for y in range(wide // NZ):
        for z in range(NZ):
            column = y * NZ + z
            for step, weight in ((1, -16.0), (-1, -16.0), (2, 1.0), (-2, 1.0)):
                matrix[y * NZ + (z + step) % NZ, column] += weight
                row = y + step
                if row < 0:
                    row += 6
                elif row >= 4:
                    row += 2
                matrix[row * NZ + z, column] += weight
    return matrix.astype(ml_dtypes.bfloat16)


def filter_kernel(space, layers, tiles, chunk, pitch, x_ref, m_ref, *refs):
    f0, f1, coef, mm, hi, lo = refs[-6:]
    rows = tiles * layers
    here = lax.axis_index("space")

    def slab_of(s):
        slab = here + s
        return jnp.where(slab >= space, slab - space, slab)

    if pitch > chunk:
        out_refs, joined = refs[:space], refs[space]
        for s in range(space):
            first = pl.multiple_of((slab_of(s) * pitch + chunk) * rows, rows)
            joined[s * rows : (s + 1) * rows, :] = x_ref[pl.ds(first, rows), :]
    else:
        joined, out_refs = refs[0], refs[1 : 1 + space]
    planes = space * layers
    quads, height, wide = f0.shape

    def put(f, j, v):
        f[j] = v
        top = v.astype(jnp.bfloat16)
        hi[j] = top
        lo[j] = (v - top.astype(jnp.float32)).astype(jnp.bfloat16)

    for j in range(quads):
        columns = []
        for half in range(2):
            column = []
            for p in range(planes):
                s, l = divmod(p, layers)
                row = (2 * j + half) * layers + l
                column.append(x_ref[pl.ds(slab_of(s) * (pitch * rows) + row, chunk, stride=rows), :])
                w = joined[s * rows + row : s * rows + row + 1, :]
                coef[j, p * chunk : (p + 1) * chunk, half * LANES : (half + 1) * LANES] = jnp.broadcast_to(
                    0.5 * w - 1.125, (chunk, LANES)
                )
            columns.append(jnp.concatenate(column, axis=0))
        put(f0, j, jnp.concatenate(columns, axis=1))

    def beside(a):
        before = jnp.concatenate([a[quads - 1 :], a[: quads - 1]], axis=0)
        after = jnp.concatenate([a[1:], a[:1]], axis=0)
        return jnp.concatenate([before[:, :, LANES:], after[:, :, :LANES]], axis=2)

    def product():
        top, rest = hi[...], lo[...]
        left = jnp.concatenate([top, beside(top), rest, beside(rest)], axis=2).reshape(quads * height, 4 * wide)
        right = jnp.concatenate([m_ref[...], m_ref[...]], axis=0)
        got = lax.dot_general(left, right, (((1,), (0,)), ((), ())), preferred_element_type=jnp.float32)
        mm[...] = got.reshape(quads, height, wide)

    def stencil(f, j):
        v = f[j]

        def moved(k):
            k = k % planes * chunk
            return jnp.concatenate([v[k:], v[:k]], axis=0) if k else v

        return v, (mm[j] + (moved(2) + moved(-2))) - 16.0 * (moved(1) + moved(-1))

    product()
    for j in range(quads):
        v, s = stencil(f0, j)
        put(f1, j, (1.0 / 96.0) * s + 0.5 * (coef[j] * v))
    product()
    for j in range(quads):
        v, s = stencil(f1, j)
        put(f0, j, ((1.0 / 48.0) * s + coef[j] * v) - f0[j])
    product()
    for j in range(quads):
        v, s = stencil(f0, j)
        y = ((1.0 / 48.0) * s + coef[j] * v) - f1[j]
        for p in range(planes):
            for half in range(2):
                block = y[p * chunk : (p + 1) * chunk, half * LANES : (half + 1) * LANES]
                out_refs[p // layers][(2 * j + half) * layers + p % layers] = block


VMEM_SPEC = pl.BlockSpec(memory_space=pltpu.VMEM)


def run_filter(x, matrix, joined, space, layers, tiles, chunk):
    rows = tiles * layers
    planes = space * layers
    pitch = x.shape[0] // (space * rows)
    shape = (tiles // 2, planes * chunk, 2 * LANES)
    out_shape = [jax.ShapeDtypeStruct((rows, chunk, LANES), jnp.float32)] * space
    if not joined:
        out_shape.append(jax.ShapeDtypeStruct((space * rows, LANES), jnp.float32))
    return pl.pallas_call(
        functools.partial(filter_kernel, space, layers, tiles, chunk, pitch),
        out_shape=out_shape,
        in_specs=[VMEM_SPEC] * (2 + len(joined)),
        out_specs=[VMEM_SPEC] * len(out_shape),
        scratch_shapes=[pltpu.VMEM(shape, jnp.float32)] * 4 + [pltpu.VMEM(shape, jnp.bfloat16)] * 2,
        compiler_params=pltpu.CompilerParams(vmem_limit_bytes=VMEM_LIMIT),
        cost_estimate=pl.CostEstimate(
            flops=50 * planes * tiles * SUBLANES * LANES,
            bytes_accessed=2 * planes * tiles * chunk * LANES * 4,
            transcendentals=0,
        ),
        name="filter",
    )(x, matrix, *joined)


def partner(index, size, k, forward=True):
    if size & (size - 1) == 0:
        return index ^ k
    moved = index + k if forward else index - k + size
    return jnp.where(moved >= size, moved - size, moved)


def exchange(x, axis, k, pitch=1):
    size = lax.axis_size(axis) // pitch
    power = size & (size - 1) == 0
    pairs = []
    for i in range(size):
        target = i ^ k if power else (i + k) % size
        pairs += [(i * pitch + low, target * pitch + low) for low in range(pitch)]
    return lax.ppermute(x, axis, pairs)


def pack_kernel(space, band, share, size, *refs):
    blocks, outs = refs[:space], refs[space:]
    here, mine = lax.axis_index("space"), lax.axis_index("band")
    for k, block in enumerate(blocks):
        group = here - k
        group = jnp.where(group < 0, group + space, group)
        first = pl.multiple_of(group * size, size)
        for step in range(band):
            out = outs[0].at[step] if len(outs) == 1 else outs[step]
            target = step if len(outs) == 1 else partner(mine, band, step)
            for q in range(share):
                out[pl.ds(first, size), q * LANES : (q + 1) * LANES] = block[target * share + q]


def pack(blocks, space, band, share, size, apart):
    shape = (space * size, share * LANES)
    out_shape = [jax.ShapeDtypeStruct(shape, jnp.float32)] * band
    if not apart:
        out_shape = [jax.ShapeDtypeStruct((band,) + shape, jnp.float32)]
    return pl.pallas_call(
        functools.partial(pack_kernel, space, band, share, size),
        out_shape=out_shape,
        in_specs=[VMEM_SPEC] * space,
        out_specs=[VMEM_SPEC] * len(out_shape),
        compiler_params=pltpu.CompilerParams(vmem_limit_bytes=VMEM_LIMIT),
        cost_estimate=pl.CostEstimate(
            flops=0, bytes_accessed=8 * band * space * size * share * LANES, transcendentals=0
        ),
        name="pack",
    )(*blocks)


def unpack_kernel(space, rows, own, sizes, *refs):
    blocks, out = refs[:-1], refs[-1]
    here = lax.axis_index("space")
    for n, block in enumerate(blocks):
        c, k = divmod(n, space)
        group = here - k
        group = jnp.where(group < 0, group + space, group)
        first = (group * own + sum(sizes[:c])) * rows
        for row in range(rows):
            out[pl.ds(first + row, sizes[c], stride=rows), :] = block[row]


def unpack(blocks, space, rows, sizes):
    own = sum(sizes)
    count = own * space
    return pl.pallas_call(
        functools.partial(unpack_kernel, space, rows, own, sizes),
        out_shape=jax.ShapeDtypeStruct((count * rows, LANES), jnp.float32),
        in_specs=[VMEM_SPEC] * len(blocks),
        out_specs=VMEM_SPEC,
        compiler_params=pltpu.CompilerParams(vmem_limit_bytes=VMEM_LIMIT),
        cost_estimate=pl.CostEstimate(flops=0, bytes_accessed=8 * count * rows * LANES, transcendentals=0),
        name="unpack",
    )(*blocks)


def half_product(band, count, which, hi, lo, first, out):
    def picked(x):
        return jnp.concatenate([x[2 * z + which] for z in range(band // 2)], axis=0)

    def dot(a, b):
        return lax.dot_general(a, b, (((1,), (1,)), ((), ())), preferred_element_type=jnp.float32)

    cells = hi.shape[-1]
    left_hi, left_lo = picked(hi), picked(lo)
    width = out.shape[1]
    bands = slice(first // count, (first + width) // count)
    right_hi = hi[bands].reshape(width, cells)
    right_lo = lo[bands].reshape(width, cells)
    for c in range(0, width, 256):
        columns = slice(c, min(c + 256, width))
        top, rest = right_hi[columns], right_lo[columns]
        out[:, columns] = dot(left_hi, top) + (dot(left_hi, rest) + dot(left_lo, top))


def gram_kernel(band, count, space, places, *refs):
    parts, (*outs, hi, lo, wide) = list(refs[: -3 - PARTS]), refs[-3 - PARTS :]
    own = count // space
    mine = lax.axis_index("band")
    for offset, size, apart in places:
        taken = [parts.pop(0) for _ in range(band)] if apart else parts.pop(0)
        for step in range(band):
            source = partner(mine, band, step, forward=False) if apart else step
            for g in range(space):
                wide[source, g * own + offset : g * own + offset + size, :] = taken[step][g * size : (g + 1) * size, :]
    for b in range(band):
        top = wide[b].astype(jnp.bfloat16)
        hi[b] = top
        lo[b] = (wide[b] - top.astype(jnp.float32)).astype(jnp.bfloat16)
    for n, out in enumerate(outs):
        half_product(band, count, 1 - mine % 2, hi, lo, n * out.shape[1], out)


def own_gram_kernel(band, count, first, hi, lo, out):
    half_product(band, count, lax.axis_index("band") % 2, hi, lo, first, out)


def gram(parts, band, count, space, places):
    cells = parts[0].shape[-1]
    half = jax.ShapeDtypeStruct((band // 2 * count, band * count // PARTS), jnp.float32)
    narrow = jax.ShapeDtypeStruct((band, count, cells), jnp.bfloat16)
    return pl.pallas_call(
        functools.partial(gram_kernel, band, count, space, places),
        out_shape=[half] * PARTS + [narrow, narrow],
        in_specs=[VMEM_SPEC] * len(parts),
        out_specs=[VMEM_SPEC] * (PARTS + 2),
        scratch_shapes=[pltpu.VMEM((band, count, cells), jnp.float32)],
        compiler_params=pltpu.CompilerParams(vmem_limit_bytes=VMEM_LIMIT),
        cost_estimate=pl.CostEstimate(
            flops=3 * band * band * count * count * cells,
            bytes_accessed=4 * band * count * (cells + band * count // 2),
            transcendentals=0,
        ),
        name="gram",
    )(*parts)


def own_gram(hi, lo, first, width):
    band, count, cells = hi.shape
    return pl.pallas_call(
        functools.partial(own_gram_kernel, band, count, first),
        out_shape=jax.ShapeDtypeStruct((band // 2 * count, width), jnp.float32),
        in_specs=[VMEM_SPEC] * 2,
        out_specs=VMEM_SPEC,
        compiler_params=pltpu.CompilerParams(vmem_limit_bytes=VMEM_LIMIT),
        cost_estimate=pl.CostEstimate(
            flops=3 * band * count * width * cells, bytes_accessed=4 * band * count * cells, transcendentals=0
        ),
        name="own_gram",
    )(hi, lo)


def combine_kernel(space, a_ref, b_ref, *outs):
    for k, out in enumerate(outs):
        group = lax.axis_index("space") + k
        group = jnp.where(group >= space, group - space, group)
        for z in range(out.shape[0]):
            out[z] = a_ref[z, group] + b_ref[z, group]


def combine(a, b):
    pairs, space, own, columns = a.shape
    return pl.pallas_call(
        functools.partial(combine_kernel, space),
        out_shape=[jax.ShapeDtypeStruct((pairs, own, columns), jnp.float32)] * space,
        in_specs=[VMEM_SPEC] * 2,
        out_specs=[VMEM_SPEC] * space,
        compiler_params=pltpu.CompilerParams(vmem_limit_bytes=VMEM_LIMIT),
        cost_estimate=pl.CostEstimate(flops=a.size, bytes_accessed=12 * a.size, transcendentals=0),
        name="combine",
    )(a, b)


def place_kernel(space, *refs):
    parts, out = refs[:-1], refs[-1]
    width = parts[0].shape[1]
    for n, part in enumerate(parts):
        h, k = divmod(n, space)
        group = lax.axis_index("space") - k
        group = jnp.where(group < 0, group + space, group)
        out[group, :, h * width : (h + 1) * width] = part[...]


def place(parts, space):
    own, width = parts[0].shape
    columns = width * len(parts) // space
    return pl.pallas_call(
        functools.partial(place_kernel, space),
        out_shape=jax.ShapeDtypeStruct((space, own, columns), jnp.float32),
        in_specs=[VMEM_SPEC] * len(parts),
        out_specs=VMEM_SPEC,
        compiler_params=pltpu.CompilerParams(vmem_limit_bytes=VMEM_LIMIT),
        cost_estimate=pl.CostEstimate(flops=0, bytes_accessed=8 * space * own * columns, transcendentals=0),
        name="place",
    )(*parts)


def rotate(x, axis, step):
    size = lax.axis_size(axis)
    return lax.ppermute(x, axis, [(i, (i + step) % size) for i in range(size)])


def shards(orbitals, potential):
    space = lax.axis_size("space")
    band = lax.axis_size("band")
    count, layers, plane = orbitals.shape
    tiles = plane // LANES
    rows = tiles * layers
    share = rows // band
    own = count // space
    chunk = max(c for c in range(1, SUBLANES + 1) if own % c == 0)
    sizes = [chunk] if own == chunk else [chunk, own - chunk]

    def as_rows(x):
        n = x.shape[0]
        return x.reshape(n, layers, tiles, LANES).transpose(0, 2, 1, 3).reshape(n * rows, LANES)

    matrix = jnp.asarray(plane_matrix())
    def over_space(x):
        x = x.reshape((-1,) + x.shape[2:])
        return lax.all_to_all(x, "space", split_axis=0, concat_axis=0, tiled=True)

    by_group = orbitals.reshape(space, own, layers, plane)
    slab_v = jnp.broadcast_to(potential[None, None], (space, 1, layers, plane))
    arrived = [over_space(jnp.concatenate([by_group[:, :chunk], slab_v], axis=1))]
    if len(sizes) > 1:
        arrived[0], late = lax.optimization_barrier((arrived[0], by_group[:, chunk:]))
        arrived.append(over_space(late))

    joined = []
    made = []
    for size, x in zip(sizes, arrived):
        outs = run_filter(as_rows(x), matrix, joined, space, layers, tiles, size)
        joined = joined or [outs[-1]]
        made.append([outs[0]] + [rotate(outs[k], "space", k) for k in range(1, space)])
    head = pack(made[0], space, band, share, sizes[0], False)[0]
    head = lax.all_to_all(head, "band", split_axis=0, concat_axis=0, tiled=True)
    parts = [head]
    places = [(0, sizes[0], False)]
    if len(made) > 1:
        packed = pack(made[1], space, band, share, sizes[1], True)
        got = {0: packed[0]}
        for k in reversed(range(1, band)):
            got[k] = exchange(packed[k], "band", k)
        parts += [got[k] for k in range(band)]
        places.append((sizes[0], sizes[1], True))
        parts[0], made[0][0] = lax.optimization_barrier((parts[0], made[0][0]))

    result = unpack(sum(made, []), space, rows, sizes)
    parts[-1], result = lax.optimization_barrier((parts[-1], result))
    result = result.reshape(count, tiles, layers, LANES).transpose(0, 2, 1, 3).reshape(count, layers, plane)

    pairs = band // 2
    pair = lax.axis_index("band") // 2
    scale = 1.0 / (layers * space * plane)

    *others, hi, lo = gram(parts, band, count, space, places)
    others = [lax.ppermute(x, "band", [(i, i ^ 1) for i in range(band)]) for x in others]
    width = band * count // PARTS
    split = (pairs, space, own, width)
    placed = []
    for h in range(PARTS):
        sums = combine(own_gram(hi, lo, h * width, width).reshape(split), others[h].reshape(split))
        sums, hi = lax.optimization_barrier((sums, hi))
        mine = sums[0]
        for k in range(1, space):
            mine = mine + rotate(sums[k], "space", k)
        final = lax.dynamic_index_in_dim(mine, pair, 0, keepdims=False)
        for k in range(1, pairs):
            sent = lax.dynamic_index_in_dim(mine, partner(pair, pairs, k), 0, keepdims=False)
            final = final + exchange(sent, "band", k, 2)
        final = final * scale
        placed += [final] + [rotate(final, "space", k) for k in range(1, space)]
    return result, place(placed, space).reshape(count, band * count)


def solution(mesh):
    return jax.shard_map(
        shards,
        mesh=mesh,
        in_specs=(P("band", "space", None), P("space", None)),
        out_specs=(P("band", "space", None), P("band", None)),
        check_vma=False,
    )
```
